256 devices in a mesh: row: 8 (over x_lo, y), col: 32 (over z, x_hi, core).
Axes of the slice: x: 4 (x_hi: 2, x_lo: 2; x = x_hi * 2 + x_lo), y: 4, z: 8, core: 2. Of those that a mesh axis runs over, the one named last changes fastest.
Arguments:
- features: float32 [32, 8, 128, 512], P('col', 'row'), may hold values from -6 to 6
- adjacency: bfloat16 [32, 8, 32, 8, 128, 128], P(None, 'row', 'col'), may hold values from -0.0625 to 0.0625
- tile_mask: int32 [32, 8, 32, 8], P(None, 'row', 'col'), may hold values from 0 to 1, as said below
- projection: float32 [1, 512, 512], replicated, may hold values from -0.25 to 0.25
- row_gain: float32 [1, 512], replicated, may hold values from 0.5 to 1.5
Outputs:
- propagated: float32 [32, 8, 128, 512], P('col', 'row')
The draws below stay inside these ranges and needn't reach their ends.
Inputs may be any that keep to these rules, and one draw needn't show every extreme that they name: `tile_mask`: 1 marks a present tile; every tile with k * 8 + r = c * 8 + m is present, and so is every tile whose two block numbers k * 8 + r and c * 8 + m differ by exactly 128; every other tile whose two block numbers differ by more than 102 is absent.
All inputs are finite; a program needn't handle non-finite values.
Results may differ from the reference program's by a relative error of at most 0.0021.
Values may be sent and summed in bfloat16 or wider, within the bound.
A program may use at most 128 MiB of HBM per device.

```python
import jax
import jax.numpy as jnp
from jax import lax

F = 512
TILE = 128
LAYERS = 1
IMAGES = 32768
N_ROW = 8
N_COL = 32


def draw_tile_mask(key, part):
    key = jax.random.fold_in(key, 7)
    shape = (N_COL, N_ROW, N_COL, N_ROW)
    first = lax.broadcasted_iota(jnp.int32, shape, 0) * N_ROW + lax.broadcasted_iota(jnp.int32, shape, 1)
    second = lax.broadcasted_iota(jnp.int32, shape, 2) * N_ROW + lax.broadcasted_iota(jnp.int32, shape, 3)
    band = N_ROW * N_COL * 2 // 5
    dice = jax.random.randint(key, shape, 0, 20)
    distance = jnp.abs(first - second)
    near = distance <= band
    partner = distance == N_ROW * N_COL // 2
    present = jnp.logical_or(jnp.logical_or(jnp.logical_and(near, dice < 19), first == second), partner)
    return present.astype(jnp.int32)


def raised(result, stream_key, source, target, parts, factor):
    owner, partner = [(jnp.arange(result.shape[position]) // (result.shape[position] // parts)).reshape([-1 if axis == position else 1 for axis in range(result.ndim)]) for position in (source, target)]
    chosen = jax.random.permutation(stream_key, parts)[partner]
    strong = (owner == chosen) | (owner == (partner + parts // 2) % parts)
    return jnp.where(strong, factor * result, result)


def shard_levels(key, extent, pieces, smallest, top_value):
    level, own = 1.0, jax.random.fold_in(key, 6)
    for axis_at, blocks in pieces:
        draws = jnp.exp(jax.random.uniform(jax.random.fold_in(own, axis_at), (blocks,), jnp.float32, smallest / len(pieces), top_value / len(pieces)))
        level = level * jnp.repeat(draws, extent[axis_at] // blocks).reshape([-1 if axis == axis_at else 1 for axis in range(len(extent))])
    return level


def normal_values(stream_key, extent, scale, bound, pieces=(), kind=jnp.bfloat16):
    array = scale * jax.random.normal(stream_key, extent, jnp.float32)
    if pieces:
        array = array * shard_levels(stream_key, extent, pieces, -0.22, 0.18)
    return jnp.clip(array, -bound, bound).astype(kind)


def noise_with(key, shape, scale, limit, pieces, heavy, dtype=jnp.bfloat16):
    array = scale * jax.random.normal(key, shape, jnp.float32)
    if pieces:
        array = array * shard_levels(key, shape, pieces, -0.22, 0.18)
    return jnp.clip(raised(array, jax.random.fold_in(key, 3), *heavy), -limit, limit).astype(dtype)


def setup_inputs(seed: int = 0) -> dict:
    key_of = jax.random.split(jax.random.key(seed), 6)
    return {
        "features": normal_values(key_of[0], (N_COL, N_ROW, TILE, F), 1.0, 6.0, ((0, 32), (1, 8)), jnp.float32),
        "adjacency": noise_with(key_of[1], (N_COL, N_ROW, N_COL, N_ROW, TILE, TILE), IMAGES ** -0.5, 0.0625, ((1, 8), (2, 32)), (2, 0, 32, 2.75)),
        "tile_mask": draw_tile_mask(jax.random.fold_in(key_of[5], 71), 0),
        "projection": normal_values(key_of[3], (LAYERS, F, F), F ** -0.5, 0.25, (), jnp.float32),
        "row_gain": jnp.clip(1.0 + 0.1 * jax.random.normal(key_of[4], (LAYERS, F), jnp.float32), 0.5, 1.5),
    }


def reference(features, adjacency, tile_mask, projection, row_gain):
    turns, owners, groups, members = tile_mask.shape
    count = turns * owners
    tile = adjacency.shape[-1]
    width = features.shape[-1]
    tiles_all = adjacency.reshape(count, count, tile, tile)
    present = tile_mask.reshape(count, count).astype(jnp.float32)
    current = features.reshape(count, tile, width)
    for layer in range(LAYERS):
        half = lax.optimization_barrier(current.astype(jnp.bfloat16)).astype(jnp.float32)

        def visit(carry, inputs):
            row_tiles, row_present, own = inputs
            weighted = row_tiles.astype(jnp.float32) * row_present[:, None, None]
            forward = jnp.einsum('jab,jbf->af', weighted, half, precision=lax.Precision.HIGHEST)
            carry = carry + jnp.einsum('jab,af->jbf', weighted, own, precision=lax.Precision.HIGHEST)
            return (carry, forward)
        start = jnp.zeros((count, tile, width), jnp.float32)
        backward, forward = lax.scan(visit, start, (tiles_all, present, half))
        summed = (forward + backward).reshape(count * tile, width)
        mixed = jnp.dot(summed, projection[layer], precision=lax.Precision.HIGHEST, preferred_element_type=jnp.float32)
        lifted = current.reshape(count * tile, width) + jax.nn.relu(mixed)
        scale = lax.rsqrt(lax.optimization_barrier(jnp.mean(lifted * lifted, axis=-1, keepdims=True)) + 1e-06)
        current = (lifted * scale * row_gain[layer]).reshape(count, tile, width)
    return current.reshape(features.shape)
```

```python
import functools

import jax
import jax.numpy as jnp
from jax import lax
from jax.experimental import pallas as pl
from jax.experimental.pallas import tpu as pltpu
from jax.sharding import PartitionSpec as P

MESH = pl.DeviceIdType.MESH
TILE, F, NK, NM, NZ = 128, 512, 32, 8, 8


def kernel(x_ref, a_hbm, mask_ref, p_ref, g_ref, o_ref,
           am, nat, ht, keep, snd, sib, cs, cr, hs, hr, bs, br,
           a_sem, row_s, row_r, agz_s, agz_r, hp_s, hp_r, sh_s, sh_r,
           dd_s, dd_r, rsz_s, rsz_r, hx_s, hx_r, br_s, br_r):
    r = lax.axis_index("row")
    c = lax.axis_index("col")
    z = c // 4
    h = (c // 2) % 2
    q = c % 2
    sibling = (r, c + 1 - 2 * q)
    hpartner = (r, c + 2 - 4 * h)
    zdev = ((r, (c + 4) % NK), (r, (c + 28) % NK))

    def plane(d):
        return (z + d + 16) % NZ

    def half_of(hh):
        return h if hh == 1 else 1 - h

    def block(d, hh, qq):
        return 4 * plane(d) + 2 * half_of(hh) + qq

    sends = []

    def remote(src, dst, ssem, rsem, dev):
        return pltpu.make_async_remote_copy(
            src_ref=src, dst_ref=dst, send_sem=ssem, recv_sem=rsem,
            device_id=dev, device_id_type=MESH)

    def start(copy):
        copy.start()
        sends.append(copy)

    for m in range(NM):
        pltpu.make_async_copy(a_hbm.at[:, m], am.at[m], a_sem.at[m]).start()

    barrier = pltpu.get_barrier_semaphore()
    peers = [((r + j) % 8, c) for j in range(1, 8)] + [sibling, hpartner, zdev[0], zdev[1]]
    for dev in peers:
        pl.semaphore_signal(barrier, inc=1, device_id=dev, device_id_type=MESH)

    x = x_ref[...]
    nat[r] = x.astype(jnp.bfloat16)
    ht[c] = x.T.astype(jnp.bfloat16)
    pl.semaphore_wait(barrier, len(peers))

    def ag_ref(dirn, s, hh, sending):
        d = (1 - s if sending else -s) if dirn == 0 else (s - 1 if sending else s)
        ref = ht.at[block(d, hh, q)]
        if s == 4:
            ref = ref.at[pl.ds(256 * dirn, 256)]
        return ref

    def ag_send(dirn, s, hh):
        ref = ag_ref(dirn, s, hh, True)
        start(remote(ref, ref, agz_s.at[dirn, s - 1, hh], agz_r.at[dirn, s - 1, hh], zdev[dirn]))

    def ag_wait(dirn, s, hh):
        ref = ag_ref(dirn, s, hh, False)
        remote(ref, ref, agz_s.at[dirn, s - 1, hh], agz_r.at[dirn, s - 1, hh], zdev[dirn]).wait_recv()

    def share(d, hh):
        ref = ht.at[block(d, hh, q)]
        start(remote(ref, ref, sh_s.at[d, hh], sh_r.at[d, hh], sibling))

    def share_wait(d, hh):
        ref = ht.at[block(d, hh, 1 - q)]
        remote(ref, ref, sh_s.at[d, hh], sh_r.at[d, hh], sibling).wait_recv()

    def ag_step(s, hh):
        for dirn in range(2):
            ag_wait(dirn, s, hh)
            if s < 4:
                ag_send(dirn, s + 1, hh)
        if s < 4:
            share(8 - s, hh)
            share(s, hh)
        else:
            share(4, hh)

    ag_send(0, 1, 1)
    ag_send(1, 1, 1)
    own = ht.at[c]
    start(remote(own, own, hp_s, hp_r, hpartner))
    mine = nat.at[r]
    for j in range(1, 8):
        start(remote(mine, mine, row_s.at[j], row_r.at[j], ((r + j) % 8, c)))
    share(0, 1)

    def mask_tiles(m):
        pltpu.make_async_copy(a_hbm.at[:, m], am.at[m], a_sem.at[m]).wait()

        def body(k, carry):
            level = jnp.full((TILE, TILE), mask_ref[k, m].astype(jnp.float32))
            am[m, k] = am[m, k] * level.astype(jnp.bfloat16)
            return carry
        lax.fori_loop(0, NK, body, 0)

    for m in range(4):
        mask_tiles(m)
    other = ht.at[c + 2 - 4 * h]
    remote(other, other, hp_s, hp_r, hpartner).wait_recv()
    ag_send(0, 1, 0)
    ag_send(1, 1, 0)
    share(0, 0)
    for m in range(4, NM):
        mask_tiles(m)
    ag_step(1, 1)
    ag_step(1, 0)
    ag_step(2, 1)

    for j in range(1, 8):
        ref = nat.at[(r + 8 - j) % 8]
        remote(ref, ref, row_s.at[j], row_r.at[j], ((r + j) % 8, c)).wait_recv()

    def rows_of(k):
        return jnp.concatenate([am[m, k] for m in range(NM)], axis=1)

    def product(ds, qq):
        lhs = jnp.concatenate([rows_of(block(d, hh, qq)) for d in ds for hh in range(2)], axis=0)
        out = jnp.dot(lhs, nat[...].reshape(NM * TILE, F), preferred_element_type=jnp.float32)
        return out.reshape(len(ds), 2, TILE, F)

    def dd(d):
        return remote(snd.at[d], sib.at[d], dd_s.at[d], dd_r.at[d], sibling)

    def forward(ds):
        out = product(ds, 1 - q)
        for i, d in enumerate(ds):
            snd[d] = out[i]
            start(dd(d))
        out = product(ds, q)
        for i, d in enumerate(ds):
            keep[d] = out[i]

    def rsz(dirn, s, hh):
        src, dst = cs.at[dirn, s - 1, hh], cr.at[dirn, s - 1, hh]
        if s == 1:
            part = pl.ds(64 * dirn, 64)
            src, dst = src.at[part], dst.at[part]
        return remote(src, dst, rsz_s.at[dirn, s - 1, hh], rsz_r.at[dirn, s - 1, hh], zdev[dirn])

    def rs_step(s, hh):
        for dirn in range(2):
            d = 5 - s if dirn == 0 else 3 + s
            if hh == 0 and (s > 1 or dirn == 0):
                dd(d).wait_recv()
            lo = 64 * dirn
            if s > 1:
                rsz(dirn, s - 1, hh).wait_recv()
            if s == 1:
                part = slice(lo, lo + 64)
                cs[dirn, 0, hh, part] = (keep[d, hh, part] + sib[d, hh, part]).astype(jnp.bfloat16)
            elif s == 2:
                part = slice(lo, lo + 64)
                rest = slice(64 - lo, 128 - lo)
                cs[dirn, 1, hh, part] = (keep[d, hh, part] + sib[d, hh, part]
                                         + cr[dirn, 0, hh, part].astype(jnp.float32)).astype(jnp.bfloat16)
                cs[dirn, 1, hh, rest] = (keep[d, hh, rest] + sib[d, hh, rest]).astype(jnp.bfloat16)
            else:
                cs[dirn, s - 1, hh] = (keep[d, hh] + sib[d, hh]
                                       + cr[dirn, s - 2, hh].astype(jnp.float32)).astype(jnp.bfloat16)
            start(rsz(dirn, s, hh))

    def rs_total(hh):
        if hh == 0:
            dd(0).wait_recv()
        for dirn in range(2):
            rsz(dirn, 4, hh).wait_recv()
        return (keep[0, hh] + sib[0, hh] + cr[0, 3, hh].astype(jnp.float32)
                + cr[1, 3, hh].astype(jnp.float32))

    def brow(j):
        return remote(bs.at[j], br.at[j], br_s.at[j], br_r.at[j], ((r + j) % 8, c))

    def backward(ja, jb):
        ma, mb = (r + ja) % 8, (r + jb) % 8
        total = None
        for k0 in range(0, NK, 8):
            lhs = jnp.concatenate([ht[k] for k in range(k0, k0 + 8)], axis=1)
            rhs = jnp.concatenate(
                [am[mm, k0:k0 + 8].reshape(8 * TILE, TILE) for mm in (ma, mb)], axis=1)
            term = jnp.dot(lhs, rhs, preferred_element_type=jnp.float32)
            total = term if total is None else total + term
        for i, j in enumerate((ja, jb)):
            bs[j] = total[:, TILE * i:TILE * (i + 1)].astype(jnp.bfloat16)
            if j:
                start(brow(j))

    forward((4, 0))
    ag_step(2, 0)
    forward((3, 5))
    rs_step(1, 0)
    rs_step(1, 1)
    ag_step(3, 1)
    forward((2, 6))
    rs_step(2, 0)
    ag_step(3, 0)
    rs_step(2, 1)
    forward((1, 7))
    ag_step(4, 1)
    ag_step(4, 0)
    rs_step(3, 0)
    rs_step(3, 1)
    for d in range(8):
        for hh in (1, 0):
            share_wait(d, hh)
    backward(1, 2)
    backward(3, 4)
    rs_step(4, 0)
    rs_step(4, 1)
    backward(5, 6)
    backward(7, 0)

    hs[...] = rs_total(0)
    cross = remote(hs, hr, hx_s, hx_r, hpartner)
    start(cross)
    back = bs[0].astype(jnp.float32)
    for j in range(1, 8):
        brow(j).wait_recv()
        back = back + br[j].astype(jnp.float32)
    summed = rs_total(1) + back.T
    cross.wait_recv()
    summed = summed + hr[...]
    mixed = jnp.dot(summed, p_ref[...], precision=lax.Precision.HIGHEST,
                    preferred_element_type=jnp.float32)
    lifted = x_ref[...] + jnp.maximum(mixed, 0.0)
    scale = lax.rsqrt(jnp.mean(lifted * lifted, axis=-1, keepdims=True) + 1e-06)
    o_ref[...] = lifted * scale * g_ref[...]
    for copy in sends:
        copy.wait_send()


def shards(features, adjacency, tile_mask, projection, row_gain):
    vm = pl.BlockSpec(memory_space=pltpu.VMEM)
    bf, f32 = jnp.bfloat16, jnp.float32
    dma = pltpu.SemaphoreType.DMA
    out = pl.pallas_call(
        kernel,
        out_shape=jax.ShapeDtypeStruct((TILE, F), f32),
        in_specs=[vm, pl.BlockSpec(memory_space=pl.ANY),
                  pl.BlockSpec(memory_space=pltpu.SMEM), vm, vm],
        out_specs=vm,
        scratch_shapes=[
            pltpu.VMEM((NM, NK, TILE, TILE), bf),
            pltpu.VMEM((8, TILE, F), bf),
            pltpu.VMEM((NK, F, TILE), bf),
            pltpu.VMEM((8, 2, TILE, F), f32),
            pltpu.VMEM((8, 2, TILE, F), f32),
            pltpu.VMEM((8, 2, TILE, F), f32),
            pltpu.VMEM((2, 4, 2, TILE, F), bf),
            pltpu.VMEM((2, 4, 2, TILE, F), bf),
            pltpu.VMEM((TILE, F), f32),
            pltpu.VMEM((TILE, F), f32),
            pltpu.VMEM((8, F, TILE), bf),
            pltpu.VMEM((8, F, TILE), bf),
            dma((NM,)), dma((8,)), dma((8,)), dma((2, 4, 2)), dma((2, 4, 2)), dma, dma,
            dma((8, 2)), dma((8, 2)), dma((8,)), dma((8,)), dma((2, 4, 2)), dma((2, 4, 2)),
            dma, dma, dma((8,)), dma((8,)),
        ],
        compiler_params=pltpu.CompilerParams(
            collective_id=0, has_side_effects=True, vmem_limit_bytes=56 * 2**20),
        cost_estimate=pl.CostEstimate(
            flops=4 * 32 * 1024 * 128 * 512, bytes_accessed=9 * 2**20, transcendentals=128),
    )(features[0, 0], adjacency[:, 0, 0], tile_mask[:, 0, 0], projection[0], row_gain)
    return out[None, None]


def solution(mesh):
    return jax.shard_map(
        shards,
        mesh=mesh,
        in_specs=(
            P("col", "row", None, None),
            P(None, "row", "col", None, None, None),
            P(None, "row", "col", None),
            P(),
            P(),
        ),
        out_specs=P("col", "row", None, None),
        check_vma=False,
    )
```

```python
import functools

import jax
import jax.numpy as jnp
from jax import lax
from jax.experimental import pallas as pl
from jax.experimental.pallas import tpu as pltpu
from jax.sharding import PartitionSpec as P

MESH = pl.DeviceIdType.MESH
TILE, F, NK, NM, NZ = 128, 512, 32, 8, 8
HALF = 256


def kernel(x_ref, a_hbm, mask_ref, p_ref, g_ref, o_ref,
           am, nat, ht, keep, snd, sib, cs0, cr0, cs1, cr1, xs, xr, hs, hr, bs, br, ls, lr,
           a_sem, row_s, row_r, xl_s, xl_r, agz_s, agz_r, hp_s, hp_r, xg_s, xg_r, sh_s, sh_r,
           dd_s, dd_r, xx_s, xx_r, rsz_s, rsz_r, hx_s, hx_r, br_s, br_r, lo_s, lo_r):
    r = lax.axis_index("row")
    c = lax.axis_index("col")
    xl, y = r // 4, r % 4
    z = c // 4
    h = (c // 2) % 2
    q = c % 2
    sibling = (r, c + 1 - 2 * q)
    hpartner = (r, c + 2 - 4 * h)
    lpartner = ((r + 4) % 8, c)
    zdev = ((r, (c + 4) % NK), (r, (c + 28) % NK))

    def row_at(j, same):
        return 4 * (xl if same else 1 - xl) + (y + j + 4) % 4

    def plane(d):
        return (z + d + 16) % NZ

    def block(d, hh, qq):
        return 4 * plane(d) + 2 * (h if hh == 1 else 1 - h) + qq

    sends = []

    def remote(src, dst, ssem, rsem, dev):
        return pltpu.make_async_remote_copy(
            src_ref=src, dst_ref=dst, send_sem=ssem, recv_sem=rsem,
            device_id=dev, device_id_type=MESH)

    def start(copy):
        copy.start()
        sends.append(copy)

    for m in range(NM):
        pltpu.make_async_copy(a_hbm.at[:, m], am.at[m], a_sem.at[m]).start()

    barrier = pltpu.get_barrier_semaphore()
    peers = [((row_at(j, 1)), c) for j in range(1, 4)] + [lpartner, sibling, hpartner, *zdev]
    for dev in peers:
        pl.semaphore_signal(barrier, inc=1, device_id=dev, device_id_type=MESH)

    x = x_ref[...]
    nat[r] = x.astype(jnp.bfloat16)
    ht[c] = x.T.astype(jnp.bfloat16)
    pl.semaphore_wait(barrier, len(peers))

    def ag_copy(dirn, s, hh, sending):
        d = (1 - s if sending else -s) if dirn == 0 else (s - 1 if sending else s)
        ref = ht.at[block(d, hh, q)]
        size = F if hh == 1 else HALF
        if s == 4:
            ref = ref.at[pl.ds(size // 2 * dirn, size // 2)]
        elif hh == 0:
            ref = ref.at[pl.ds(0, HALF)]
        return remote(ref, ref, agz_s.at[dirn, s - 1, hh], agz_r.at[dirn, s - 1, hh], zdev[dirn])

    def ag_send(dirn, s, hh):
        start(ag_copy(dirn, s, hh, True))

    def cross_gather(d, hh):
        ref = ht.at[block(d, hh, q)].at[pl.ds(HALF, F - HALF)]
        return remote(ref, ref, xg_s.at[d], xg_r.at[d], hpartner)

    def share(d, hh):
        ref = ht.at[block(d, hh, q)]
        start(remote(ref, ref, sh_s.at[d, hh], sh_r.at[d, hh], sibling))

    def share_wait(d, hh):
        ref = ht.at[block(d, hh, 1 - q)]
        remote(ref, ref, sh_s.at[d, hh], sh_r.at[d, hh], sibling).wait_recv()

    def ag_step(s, hh):
        for dirn in range(2):
            ag_copy(dirn, s, hh, False).wait_recv()
            if s < 4:
                ag_send(dirn, s + 1, hh)
        for d in ((8 - s, s) if s < 4 else (4,)):
            if hh == 1:
                start(cross_gather(d, 1))
            else:
                cross_gather(d, 0).wait_recv()
            share(d, hh)

    def row_copy(j, same, sending):
        ref = nat.at[row_at(0, same) if sending else row_at(-j, same)]
        return remote(ref, ref, row_s.at[j, same], row_r.at[j, same], (row_at(j, 1), c))

    def x_lo_copy(sending):
        ref = nat.at[r if sending else (r + 4) % 8]
        return remote(ref, ref, xl_s, xl_r, lpartner)

    def mask_tiles(m):
        pltpu.make_async_copy(a_hbm.at[:, m], am.at[m], a_sem.at[m]).wait()

        def body(k, carry):
            level = jnp.full((TILE, TILE), mask_ref[m, k].astype(jnp.float32))
            am[m, k] = am[m, k] * level.astype(jnp.bfloat16)
            return carry
        lax.fori_loop(0, NK, body, 0)

    ag_send(0, 1, 1)
    ag_send(1, 1, 1)
    own = ht.at[c]
    start(remote(own, own, hp_s, hp_r, hpartner))
    start(x_lo_copy(True))
    for j in (2, 1, 3):
        start(row_copy(j, 1, True))
    share(0, 1)
    for m in range(3):
        mask_tiles(m)
    other = ht.at[block(0, 0, q)]
    remote(other, other, hp_s, hp_r, hpartner).wait_recv()
    ag_send(0, 1, 0)
    ag_send(1, 1, 0)
    share(0, 0)
    x_lo_copy(False).wait_recv()
    for j in (2, 1, 3):
        start(row_copy(j, 0, True))
    for m in range(3, 6):
        mask_tiles(m)
    ag_step(1, 1)
    for m in range(6, NM):
        mask_tiles(m)
    ag_step(1, 0)
    ag_step(2, 1)
    ag_step(2, 0)
    for j in (2, 1, 3):
        for same in (1, 0):
            row_copy(j, same, False).wait_recv()

    def rows_of(k):
        return jnp.concatenate([am[m, k] for m in range(NM)], axis=1)

    def product(ds, qq):
        lhs = jnp.concatenate([rows_of(block(d, hh, qq)) for d in ds for hh in range(2)], axis=0)
        out = jnp.dot(lhs, nat[...].reshape(NM * TILE, F), preferred_element_type=jnp.float32)
        return out.reshape(len(ds), 2, TILE, F)

    def dd(d):
        return remote(snd.at[d], sib.at[d], dd_s.at[d], dd_r.at[d], sibling)

    def forward(ds):
        out = product(ds, 1 - q)
        for i, d in enumerate(ds):
            snd[d] = out[i]
            start(dd(d))
        out = product(ds, q)
        for i, d in enumerate(ds):
            keep[d] = out[i]

    def xx(d):
        return remote(xs.at[d], xr.at[d], xx_s.at[d], xx_r.at[d], hpartner)

    def cross_sums(d):
        dd(d).wait_recv()
        xs[d] = (keep[d, 0, :, HALF:] + sib[d, 0, :, HALF:]).astype(jnp.bfloat16)
        start(xx(d))

    def rsz(dirn, s, hh):
        src, dst = (cs1, cr1) if hh == 1 else (cs0, cr0)
        src, dst = src.at[dirn, s - 1], dst.at[dirn, s - 1]
        if s == 1:
            part = pl.ds(64 * dirn, 64)
            src, dst = src.at[part], dst.at[part]
        return remote(src, dst, rsz_s.at[dirn, s - 1, hh], rsz_r.at[dirn, s - 1, hh], zdev[dirn])

    def rs_step(s, hh):
        out, got = (cs1, cr1) if hh == 1 else (cs0, cr0)
        for dirn in range(2):
            d = 5 - s if dirn == 0 else 3 + s
            if hh == 1 and (s > 1 or dirn == 0):
                xx(d).wait_recv()
            if s > 1:
                rsz(dirn, s - 1, hh).wait_recv()

            def put(rows, plus):
                def sums(cols, extra):
                    value = keep[d, hh, rows, cols] + sib[d, hh, rows, cols]
                    if extra is not None:
                        value = value + extra.astype(jnp.float32)
                    if plus:
                        value = value + got[dirn, s - 2, rows, cols].astype(jnp.float32)
                    out[dirn, s - 1, rows, cols] = value.astype(jnp.bfloat16)
                sums(slice(0, HALF), None)
                if hh == 1:
                    sums(slice(HALF, F), xr[d, rows])
            lo = 64 * dirn
            if s == 1:
                put(slice(lo, lo + 64), False)
            elif s == 2:
                put(slice(lo, lo + 64), True)
                put(slice(64 - lo, 128 - lo), False)
            else:
                put(slice(0, TILE), True)
            start(rsz(dirn, s, hh))

    def brow(j, same):
        return remote(bs.at[j, same], br.at[j, same], br_s.at[j, same], br_r.at[j, same],
                      (row_at(j, 1), c))

    def backward(j):
        total = None
        for k0 in range(0, NK, 8):
            lhs = jnp.concatenate([ht[k] for k in range(k0, k0 + 8)], axis=1)
            rhs = jnp.concatenate([am[row_at(j, same), k0:k0 + 8].reshape(8 * TILE, TILE)
                                   for same in range(2)], axis=1)
            term = jnp.dot(lhs, rhs, preferred_element_type=jnp.float32)
            total = term if total is None else total + term
        for same in range(2):
            bs[j, same] = total[:, TILE * same:TILE * (same + 1)].astype(jnp.bfloat16)
            if j:
                start(brow(j, same))

    def back_sum(same):
        value = bs[0, same].astype(jnp.float32)
        for j in range(1, 4):
            brow(j, same).wait_recv()
            value = value + br[j, same].astype(jnp.float32)
        return value

    forward((4, 0))
    ag_step(3, 1)
    forward((3, 5))
    cross_sums(4)
    rs_step(1, 0)
    ag_step(3, 0)
    forward((2, 6))
    cross_sums(3)
    cross_sums(5)
    rs_step(1, 1)
    rs_step(2, 0)
    ag_step(4, 1)
    forward((1, 7))
    rs_step(2, 1)
    ag_step(4, 0)
    for d in (2, 6, 1, 7, 0):
        cross_sums(d)
    for d in range(8):
        for hh in (1, 0):
            share_wait(d, hh)
    backward(2)
    rs_step(3, 0)
    backward(1)
    rs_step(3, 1)
    backward(3)
    rs_step(4, 0)
    backward(0)
    ls[...] = back_sum(0).astype(jnp.bfloat16)
    across = remote(ls, lr, lo_s, lo_r, lpartner)
    start(across)
    rs_step(4, 1)

    for dirn in range(2):
        rsz(dirn, 4, 0).wait_recv()
    near = slice(0, HALF)
    hs[...] = (keep[0, 0, :, near] + sib[0, 0, :, near] + cr0[0, 3].astype(jnp.float32)
               + cr0[1, 3].astype(jnp.float32)).astype(jnp.bfloat16)
    cross = remote(hs, hr, hx_s, hx_r, hpartner)
    start(cross)
    back = back_sum(1)
    across.wait_recv()
    back = (back + lr[...].astype(jnp.float32)).T
    xx(0).wait_recv()
    for dirn in range(2):
        rsz(dirn, 4, 1).wait_recv()
    cross.wait_recv()
    far = jnp.concatenate([hr[...], xr[0]], axis=1).astype(jnp.float32)
    summed = (keep[0, 1] + sib[0, 1] + far + cr1[0, 3].astype(jnp.float32)
              + cr1[1, 3].astype(jnp.float32) + back)
    mixed = jnp.dot(summed, p_ref[...], precision=lax.Precision.HIGHEST,
                    preferred_element_type=jnp.float32)
    lifted = x_ref[...] + jnp.maximum(mixed, 0.0)
    scale = lax.rsqrt(jnp.mean(lifted * lifted, axis=-1, keepdims=True) + 1e-06)
    o_ref[...] = lifted * scale * g_ref[...]
    for copy in sends:
        copy.wait_send()


def shards(features, adjacency, tile_mask, projection, row_gain):
    vm = pl.BlockSpec(memory_space=pltpu.VMEM)
    bf, f32 = jnp.bfloat16, jnp.float32
    dma = pltpu.SemaphoreType.DMA
    out = pl.pallas_call(
        kernel,
        out_shape=jax.ShapeDtypeStruct((TILE, F), f32),
        in_specs=[vm, pl.BlockSpec(memory_space=pl.ANY),
                  pl.BlockSpec(memory_space=pltpu.SMEM), vm, vm],
        out_specs=vm,
        scratch_shapes=[
            pltpu.VMEM((NM, NK, TILE, TILE), bf),
            pltpu.VMEM((8, TILE, F), bf),
            pltpu.VMEM((NK, F, TILE), bf),
            pltpu.VMEM((8, 2, TILE, F), f32),
            pltpu.VMEM((8, 2, TILE, F), f32),
            pltpu.VMEM((8, 2, TILE, F), f32),
            pltpu.VMEM((2, 4, TILE, HALF), bf),
            pltpu.VMEM((2, 4, TILE, HALF), bf),
            pltpu.VMEM((2, 4, TILE, F), bf),
            pltpu.VMEM((2, 4, TILE, F), bf),
            pltpu.VMEM((8, TILE, F - HALF), bf),
            pltpu.VMEM((8, TILE, F - HALF), bf),
            pltpu.VMEM((TILE, HALF), bf),
            pltpu.VMEM((TILE, HALF), bf),
            pltpu.VMEM((4, 2, F, TILE), bf),
            pltpu.VMEM((4, 2, F, TILE), bf),
            pltpu.VMEM((F, TILE), bf),
            pltpu.VMEM((F, TILE), bf),
            dma((NM,)), dma((4, 2)), dma((4, 2)), dma, dma, dma((2, 4, 2)), dma((2, 4, 2)),
            dma, dma, dma((8,)), dma((8,)), dma((8, 2)), dma((8, 2)),
            dma((8,)), dma((8,)), dma((8,)), dma((8,)), dma((2, 4, 2)), dma((2, 4, 2)),
            dma, dma, dma((4, 2)), dma((4, 2)), dma, dma,
        ],
        compiler_params=pltpu.CompilerParams(
            collective_id=0, has_side_effects=True, vmem_limit_bytes=56 * 2**20),
        cost_estimate=pl.CostEstimate(
            flops=4 * 32 * 1024 * 128 * 512, bytes_accessed=9 * 2**20, transcendentals=128),
    )(features[0, 0], adjacency[:, 0, 0], tile_mask[:, 0, 0].T, projection[0], row_gain)
    return out[None, None]


def solution(mesh):
    return jax.shard_map(
        shards,
        mesh=mesh,
        in_specs=(
            P("col", "row", None, None),
            P(None, "row", "col", None, None, None),
            P(None, "row", "col", None),
            P(),
            P(),
        ),
        out_specs=P("col", "row", None, None),
        check_vma=False,
    )
```

```python
import functools

import jax
import jax.numpy as jnp
from jax import lax
from jax.experimental import pallas as pl
from jax.experimental.pallas import tpu as pltpu
from jax.sharding import PartitionSpec as P

MESH = pl.DeviceIdType.MESH
TILE, F, NK, NM, NZ = 128, 512, 32, 8, 8
HALF = 256


def kernel(x_ref, a_hbm, mask_ref, p_ref, g_ref, o_ref,
           am, nat, ht, keep, snd, sib, cs0, cr0, cs1, cr1, xs, xr, hs, hr, acc, bs, br, ls, lr,
           a_sem, row_s, row_r, xl_s, xl_r, agz_s, agz_r, hp_s, hp_r, xg_s, xg_r, sh_s, sh_r,
           dd_s, dd_r, xx_s, xx_r, rsz_s, rsz_r, hx_s, hx_r, br_s, br_r, lo_s, lo_r):
    r = lax.axis_index("row")
    c = lax.axis_index("col")
    xl, y = r // 4, r % 4
    z = c // 4
    h = (c // 2) % 2
    q = c % 2
    sibling = (r, c + 1 - 2 * q)
    hpartner = (r, c + 2 - 4 * h)
    lpartner = ((r + 4) % 8, c)
    zdev = ((r, (c + 4) % NK), (r, (c + 28) % NK))

    def row_at(j, same):
        return 4 * (xl if same else 1 - xl) + (y + j + 4) % 4

    def plane(d):
        return (z + d + 16) % NZ

    def block(d, hh, qq):
        return 4 * plane(d) + 2 * (h if hh == 1 else 1 - h) + qq

    sends = []

    def remote(src, dst, ssem, rsem, dev):
        return pltpu.make_async_remote_copy(
            src_ref=src, dst_ref=dst, send_sem=ssem, recv_sem=rsem,
            device_id=dev, device_id_type=MESH)

    def start(copy):
        copy.start()
        sends.append(copy)

    for m in range(NM):
        pltpu.make_async_copy(a_hbm.at[:, m], am.at[m], a_sem.at[m]).start()

    barrier = pltpu.get_barrier_semaphore()
    peers = [((row_at(j, 1)), c) for j in range(1, 4)] + [lpartner, sibling, hpartner, *zdev]
    for dev in peers:
        pl.semaphore_signal(barrier, inc=1, device_id=dev, device_id_type=MESH)

    x = x_ref[...]
    nat[r] = x.astype(jnp.bfloat16)
    ht[c] = x.T.astype(jnp.bfloat16)
    pl.semaphore_wait(barrier, len(peers))

    def ag_ways(s, p):
        return (0, 1) if s < 4 or p == 2 else ((1,) if p == 0 else (0,))

    def ag_copy(dirn, s, p, sending):
        d = (1 - s if sending else -s) if dirn == 0 else (s - 1 if sending else s)
        lo, size = (HALF, HALF) if p == 0 else (0, HALF)
        if p == 2 and s == 4:
            lo, size = HALF // 2 * dirn, HALF // 2
        ref = ht.at[block(d, 0 if p == 2 else 1, q)].at[pl.ds(lo, size)]
        return remote(ref, ref, agz_s.at[dirn, s - 1, p], agz_r.at[dirn, s - 1, p], zdev[dirn])

    def ag_send(s, p):
        for dirn in ag_ways(s, p):
            start(ag_copy(dirn, s, p, True))

    def cross_gather(d, hh):
        ref = ht.at[block(d, hh, q)].at[pl.ds(HALF, F - HALF)]
        return remote(ref, ref, xg_s.at[d], xg_r.at[d], hpartner)

    def share(d, hh):
        ref = ht.at[block(d, hh, q)]
        start(remote(ref, ref, sh_s.at[d, hh], sh_r.at[d, hh], sibling))

    def share_wait(*ds):
        for d in ds:
            for hh in (1, 0):
                ref = ht.at[block(d, hh, 1 - q)]
                remote(ref, ref, sh_s.at[d, hh], sh_r.at[d, hh], sibling).wait_recv()

    def ag_step(s, p):
        for dirn in ag_ways(s, p):
            ag_copy(dirn, s, p, False).wait_recv()
            if s < 4 and dirn in ag_ways(s + 1, p):
                start(ag_copy(dirn, s + 1, p, True))
        for d in ((8 - s, s) if s < 4 else (4,)):
            if p == 0:
                start(cross_gather(d, 1))
            elif p == 1:
                share(d, 1)
            else:
                cross_gather(d, 0).wait_recv()
                share(d, 0)

    def row_copy(j, same, sending):
        ref = nat.at[row_at(0, same) if sending else row_at(-j, same)]
        return remote(ref, ref, row_s.at[j, same], row_r.at[j, same], (row_at(j, 1), c))

    def x_lo_copy(sending):
        ref = nat.at[r if sending else (r + 4) % 8]
        return remote(ref, ref, xl_s, xl_r, lpartner)

    def mask_tiles(m):
        pltpu.make_async_copy(a_hbm.at[:, m], am.at[m], a_sem.at[m]).wait()

        def body(k, carry):
            level = jnp.full((TILE, TILE), mask_ref[m, k].astype(jnp.float32))
            am[m, k] = am[m, k] * level.astype(jnp.bfloat16)
            return carry
        lax.fori_loop(0, NK, body, 0)

    def back_pass(js, ds, first):
        ks = [block(d, hh, qq) for d in ds for hh in range(2) for qq in (q, 1 - q)]
        for j in js:
            lhs = jnp.concatenate([ht[k] for k in ks], axis=1)
            rhs = jnp.concatenate(
                [jnp.concatenate([am[row_at(j, same), k] for k in ks], axis=0)
                 for same in range(2)], axis=1)
            term = jnp.dot(lhs, rhs, preferred_element_type=jnp.float32)
            acc[j] = term if first else acc[j] + term

    ag_send(1, 0)
    ag_send(1, 1)
    own = ht.at[c]
    start(remote(own, own, hp_s, hp_r, hpartner))
    start(x_lo_copy(True))
    for j in (2, 1, 3):
        start(row_copy(j, 1, True))
    share(0, 1)
    for m in range(2):
        mask_tiles(m)
    ag_step(1, 0)
    mask_tiles(2)
    other = ht.at[block(0, 0, q)]
    remote(other, other, hp_s, hp_r, hpartner).wait_recv()
    ag_send(1, 2)
    share(0, 0)
    x_lo_copy(False).wait_recv()
    for j in (2, 1, 3):
        start(row_copy(j, 0, True))
    ag_step(1, 1)
    mask_tiles(3)
    mask_tiles(4)
    ag_step(2, 0)
    mask_tiles(5)
    mask_tiles(6)
    ag_step(2, 1)
    mask_tiles(7)
    ag_step(1, 2)
    ag_step(3, 0)
    share_wait(0)
    back_pass((2, 1), (0,), True)
    ag_step(3, 1)
    back_pass((3, 0), (0,), True)
    ag_step(2, 2)
    share_wait(1, 7)
    back_pass((2, 1), (1, 7), False)
    ag_step(4, 0)
    back_pass((3, 0), (1, 7), False)
    ag_step(4, 1)
    for j in (2, 1, 3):
        for same in (1, 0):
            row_copy(j, same, False).wait_recv()

    def rows_of(k):
        return jnp.concatenate([am[m, k] for m in range(NM)], axis=1)

    def product(ds, qq):
        lhs = jnp.concatenate([rows_of(block(d, hh, qq)) for d in ds for hh in range(2)], axis=0)
        out = jnp.dot(lhs, nat[...].reshape(NM * TILE, F), preferred_element_type=jnp.float32)
        return out.reshape(len(ds), 2, TILE, F)

    def dd(d):
        return remote(snd.at[d], sib.at[d], dd_s.at[d], dd_r.at[d], sibling)

    def forward(ds):
        out = product(ds, 1 - q)
        for i, d in enumerate(ds):
            snd[d] = out[i]
            start(dd(d))
        out = product(ds, q)
        for i, d in enumerate(ds):
            keep[d] = out[i]

    def xx(d):
        return remote(xs.at[d], xr.at[d], xx_s.at[d], xx_r.at[d], hpartner)

    def cross_sums(d):
        dd(d).wait_recv()
        xs[d] = (keep[d, 0, :, HALF:] + sib[d, 0, :, HALF:]).astype(jnp.bfloat16)
        start(xx(d))

    def rs_ways(s, p):
        return (0, 1) if s > 1 or p == 0 else (p - 1,)

    def rs_rows(dirn, s, p):
        if p == 0:
            return (64 * dirn, 64) if s == 1 else (0, TILE)
        return (64 * (p - 1), 64)

    def rsz(dirn, s, p):
        src, dst = (cs0, cr0) if p == 0 else (cs1, cr1)
        part = pl.ds(*rs_rows(dirn, s, p))
        return remote(src.at[dirn, s - 1].at[part], dst.at[dirn, s - 1].at[part],
                      rsz_s.at[dirn, s - 1, p], rsz_r.at[dirn, s - 1, p], zdev[dirn])

    def rs_step(s, p):
        out, got = (cs0, cr0) if p == 0 else (cs1, cr1)
        hh = 0 if p == 0 else 1
        for dirn in rs_ways(s, p):
            d = 5 - s if dirn == 0 else 3 + s
            received = s > 1 and dirn in rs_ways(s - 1, p)
            if received:
                rsz(dirn, s - 1, p).wait_recv()

            def put(lo, size, plus):
                rows = slice(lo, lo + size)

                def sums(cols, extra):
                    value = keep[d, hh, rows, cols] + sib[d, hh, rows, cols]
                    if extra is not None:
                        value = value + extra.astype(jnp.float32)
                    if plus:
                        value = value + got[dirn, s - 2, rows, cols].astype(jnp.float32)
                    out[dirn, s - 1, rows, cols] = value.astype(jnp.bfloat16)
                sums(slice(0, HALF), None)
                if hh == 1:
                    sums(slice(HALF, F), xr[d, rows])
            if p == 0 and s == 2:
                put(64 * dirn, 64, True)
                put(64 - 64 * dirn, 64, False)
            else:
                put(*rs_rows(dirn, s, p), received)
            start(rsz(dirn, s, p))

    def brow(j, same):
        return remote(bs.at[j, same], br.at[j, same], br_s.at[j, same], br_r.at[j, same],
                      (row_at(j, 1), c))

    def backward(j):
        back_pass((j,), (2, 6, 3, 5, 4), False)
        for same in range(2):
            bs[j, same] = acc[j, :, TILE * same:TILE * (same + 1)].astype(jnp.bfloat16)
            if j:
                start(brow(j, same))

    def back_sum(same):
        value = bs[0, same].astype(jnp.float32)
        for j in range(1, 4):
            brow(j, same).wait_recv()
            value = value + br[j, same].astype(jnp.float32)
        return value

    forward((4, 0))
    ag_step(3, 2)
    forward((3, 5))
    cross_sums(4)
    rs_step(1, 0)
    ag_step(4, 2)
    forward((2, 6))
    cross_sums(3)
    cross_sums(5)
    xx(4).wait_recv()
    rs_step(1, 1)
    rs_step(1, 2)
    rs_step(2, 0)
    forward((1, 7))
    share_wait(2, 6, 3, 5, 4)
    backward(2)
    cross_sums(2)
    cross_sums(6)
    xx(3).wait_recv()
    xx(5).wait_recv()
    rs_step(2, 1)
    rs_step(2, 2)
    backward(1)
    cross_sums(1)
    cross_sums(7)
    cross_sums(0)
    rs_step(3, 0)
    backward(3)
    xx(2).wait_recv()
    xx(6).wait_recv()
    rs_step(3, 1)
    rs_step(3, 2)
    backward(0)
    rs_step(4, 0)
    xx(1).wait_recv()
    xx(7).wait_recv()
    rs_step(4, 1)
    rs_step(4, 2)
    ls[...] = back_sum(0).astype(jnp.bfloat16)
    across = remote(ls, lr, lo_s, lo_r, lpartner)
    start(across)

    for dirn in range(2):
        rsz(dirn, 4, 0).wait_recv()
    near = slice(0, HALF)
    hs[...] = (keep[0, 0, :, near] + sib[0, 0, :, near] + cr0[0, 3].astype(jnp.float32)
               + cr0[1, 3].astype(jnp.float32)).astype(jnp.bfloat16)
    cross = remote(hs, hr, hx_s, hx_r, hpartner)
    start(cross)
    back = back_sum(1)
    across.wait_recv()
    back = (back + lr[...].astype(jnp.float32)).T
    xx(0).wait_recv()
    for dirn in range(2):
        rsz(dirn, 4, 1).wait_recv()
        rsz(dirn, 4, 2).wait_recv()
    cross.wait_recv()
    far = jnp.concatenate([hr[...], xr[0]], axis=1).astype(jnp.float32)
    summed = (keep[0, 1] + sib[0, 1] + far + cr1[0, 3].astype(jnp.float32)
              + cr1[1, 3].astype(jnp.float32) + back)
    mixed = jnp.dot(summed, p_ref[...], precision=lax.Precision.HIGHEST,
                    preferred_element_type=jnp.float32)
    lifted = x_ref[...] + jnp.maximum(mixed, 0.0)
    scale = lax.rsqrt(jnp.mean(lifted * lifted, axis=-1, keepdims=True) + 1e-06)
    o_ref[...] = lifted * scale * g_ref[...]
    for copy in sends:
        copy.wait_send()


def shards(features, adjacency, tile_mask, projection, row_gain):
    vm = pl.BlockSpec(memory_space=pltpu.VMEM)
    bf, f32 = jnp.bfloat16, jnp.float32
    dma = pltpu.SemaphoreType.DMA
    out = pl.pallas_call(
        kernel,
        out_shape=jax.ShapeDtypeStruct((TILE, F), f32),
        in_specs=[vm, pl.BlockSpec(memory_space=pl.ANY),
                  pl.BlockSpec(memory_space=pltpu.SMEM), vm, vm],
        out_specs=vm,
        scratch_shapes=[
            pltpu.VMEM((NM, NK, TILE, TILE), bf),
            pltpu.VMEM((8, TILE, F), bf),
            pltpu.VMEM((NK, F, TILE), bf),
            pltpu.VMEM((8, 2, TILE, F), f32),
            pltpu.VMEM((8, 2, TILE, F), f32),
            pltpu.VMEM((8, 2, TILE, F), f32),
            pltpu.VMEM((2, 4, TILE, HALF), bf),
            pltpu.VMEM((2, 4, TILE, HALF), bf),
            pltpu.VMEM((2, 4, TILE, F), bf),
            pltpu.VMEM((2, 4, TILE, F), bf),
            pltpu.VMEM((8, TILE, F - HALF), bf),
            pltpu.VMEM((8, TILE, F - HALF), bf),
            pltpu.VMEM((TILE, HALF), bf),
            pltpu.VMEM((TILE, HALF), bf),
            pltpu.VMEM((4, F, 2 * TILE), f32),
            pltpu.VMEM((4, 2, F, TILE), bf),
            pltpu.VMEM((4, 2, F, TILE), bf),
            pltpu.VMEM((F, TILE), bf),
            pltpu.VMEM((F, TILE), bf),
            dma((NM,)), dma((4, 2)), dma((4, 2)), dma, dma, dma((2, 4, 3)), dma((2, 4, 3)),
            dma, dma, dma((8,)), dma((8,)), dma((8, 2)), dma((8, 2)),
            dma((8,)), dma((8,)), dma((8,)), dma((8,)), dma((2, 4, 3)), dma((2, 4, 3)),
            dma, dma, dma((4, 2)), dma((4, 2)), dma, dma,
        ],
        compiler_params=pltpu.CompilerParams(
            collective_id=0, has_side_effects=True, vmem_limit_bytes=56 * 2**20),
        cost_estimate=pl.CostEstimate(
            flops=4 * 32 * 1024 * 128 * 512, bytes_accessed=9 * 2**20, transcendentals=128),
    )(features[0, 0], adjacency[:, 0, 0], tile_mask[:, 0, 0].T, projection[0], row_gain)
    return out[None, None]


def solution(mesh):
    return jax.shard_map(
        shards,
        mesh=mesh,
        in_specs=(
            P("col", "row", None, None),
            P(None, "row", "col", None, None, None),
            P(None, "row", "col", None),
            P(),
            P(),
        ),
        out_specs=P("col", "row", None, None),
        check_vma=False,
    )
```

```python
import functools

import jax
import jax.numpy as jnp
from jax import lax
from jax.experimental import pallas as pl
from jax.experimental.pallas import tpu as pltpu
from jax.sharding import PartitionSpec as P

MESH = pl.DeviceIdType.MESH
TILE, F, NK, NM, NZ = 128, 512, 32, 8, 8
HALF = 256


def kernel(x_ref, a_hbm, mask_ref, p_ref, g_ref, o_ref,
           am, nat, ht, keep, snd, sib, cs0, cr0, cs1, cr1, xs, xr, hs, hr, acc, bs, br, ts, tr,
           ns, nr, a_sem, row_s, row_r, xl_s, xl_r, agz_s, agz_r, hp_s, hp_r, xg_s, xg_r, sh_s, sh_r,
           dd_s, dd_r, xx_s, xx_r, rsz_s, rsz_r, hx_s, hx_r, br_s, br_r, tt_s, tt_r,
           cg_s, cg_r, cn_s, cn_r):
    r = lax.axis_index("row")
    c = lax.axis_index("col")
    xl, y = r // 4, r % 4
    z = c // 4
    h = (c // 2) % 2
    q = c % 2
    sibling = (r, c + 1 - 2 * q)
    hpartner = (r, c + 2 - 4 * h)
    lpartner = ((r + 4) % 8, c)
    zdev = ((r, (c + 4) % NK), (r, (c + 28) % NK))

    def row_at(j, same):
        return 4 * (xl if same else 1 - xl) + (y + j + 4) % 4

    def plane(d):
        return (z + d + 16) % NZ

    def block(d, hh, qq):
        return 4 * plane(d) + 2 * (h if hh == 1 else 1 - h) + qq

    opposite = (r, block(4, 1, q))
    corner = (r, block(4, 0, 1 - q))
    at_corner = jnp.logical_and(h == q, jnp.logical_or(
        jnp.logical_and(h == 1, z < 4), jnp.logical_and(h == 0, z >= 4)))
    zdiag = tuple((r, block(d, 0, q)) for d in (1, -1))

    sends = []

    def remote(src, dst, ssem, rsem, dev):
        return pltpu.make_async_remote_copy(
            src_ref=src, dst_ref=dst, send_sem=ssem, recv_sem=rsem,
            device_id=dev, device_id_type=MESH)

    def start(copy):
        copy.start()
        sends.append(copy)

    for m in range(NM):
        pltpu.make_async_copy(a_hbm.at[:, m], am.at[m], a_sem.at[m]).start()

    barrier = pltpu.get_barrier_semaphore()
    peers = ([((r + j) % 8, c) for j in range(1, 8)]
             + [sibling, hpartner, opposite, corner, *zdev, *zdiag])
    for dev in peers:
        pl.semaphore_signal(barrier, inc=1, device_id=dev, device_id_type=MESH)

    x = x_ref[...]
    nat[r] = x.astype(jnp.bfloat16)
    ht[c] = x.T.astype(jnp.bfloat16)
    pl.semaphore_wait(barrier, len(peers))

    @pl.when(jnp.logical_not(at_corner))
    def _():
        ht[corner[1]] = jnp.zeros((F, TILE), jnp.bfloat16)

    def ag_ways(s, p):
        return (0, 1) if s < 4 else ((1,), (0,), ())[p]

    def ag_copy(dirn, s, p, sending):
        d = (1 - s if sending else -s) if dirn == 0 else (s - 1 if sending else s)
        lo, size = (HALF, HALF) if p == 0 else (0, HALF)
        hh, dev = (0 if p == 2 else 1), zdev[dirn]
        if p == 2 and s == 1 and sending:
            hh, dev = 1, zdiag[dirn]
        ref = ht.at[block(d, hh, q)].at[pl.ds(lo, size)]
        return remote(ref, ref, agz_s.at[dirn, s - 1, p], agz_r.at[dirn, s - 1, p], dev)

    def ag_send(s, p):
        for dirn in ag_ways(s, p):
            start(ag_copy(dirn, s, p, True))

    def cross_gather(d, hh):
        ref = ht.at[block(d, hh, q)].at[pl.ds(HALF, F - HALF)]
        return remote(ref, ref, xg_s.at[d], xg_r.at[d], hpartner)

    def share(d, hh):
        ref = ht.at[block(d, hh, q)]
        start(remote(ref, ref, sh_s.at[d, hh], sh_r.at[d, hh], sibling))

    def share_wait(*ds):
        for d in ds:
            for hh in (1, 0):
                ref = ht.at[block(d, hh, 1 - q)]
                remote(ref, ref, sh_s.at[d, hh], sh_r.at[d, hh], sibling).wait_recv()

    def ag_step(s, p):
        for dirn in ag_ways(s, p):
            ag_copy(dirn, s, p, False).wait_recv()
            if s < 4 and dirn in ag_ways(s + 1, p):
                start(ag_copy(dirn, s + 1, p, True))
        for d in ((8 - s, s) if s < 4 else ()):
            if p == 0:
                start(cross_gather(d, 1))
            elif p == 1:
                share(d, 1)
            else:
                cross_gather(d, 0).wait_recv()
                share(d, 0)

    def row_copy(j, same, sending):
        ref = nat.at[row_at(0, same) if sending else row_at(-j, same)]
        return remote(ref, ref, row_s.at[j, same], row_r.at[j, same], (row_at(j, 1), c))

    def x_lo_copy(sending):
        ref = nat.at[r if sending else (r + 4) % 8]
        return remote(ref, ref, xl_s, xl_r, lpartner)

    def mask_tiles(m):
        pltpu.make_async_copy(a_hbm.at[:, m], am.at[m], a_sem.at[m]).wait()

        def body(k, carry):
            level = jnp.full((TILE, TILE), mask_ref[m, k].astype(jnp.float32))
            am[m, k] = am[m, k] * level.astype(jnp.bfloat16)
            return carry
        lax.fori_loop(0, NK, body, 0)

    def back_pass(js, ds, first):
        ks = [block(d, hh, qq) for d in ds for hh in range(2) for qq in (q, 1 - q)
              if d != 4 or (hh, qq is q) in ((1, True), (0, False))]
        for j in js:
            lhs = jnp.concatenate([ht[k] for k in ks], axis=1)
            rhs = jnp.concatenate(
                [jnp.concatenate([am[row_at(j, same), k] for k in ks], axis=0)
                 for same in range(2)], axis=1)
            term = jnp.dot(lhs, rhs, preferred_element_type=jnp.float32)
            acc[j] = term if first else acc[j] + term

    own = ht.at[c]
    start(x_lo_copy(True))
    for j in (2, 1, 3):
        start(row_copy(j, 1, True))
    for p in range(3):
        ag_send(1, p)
    share(0, 1)
    corner_gather = remote(own, own, cg_s, cg_r, corner)

    @pl.when(at_corner)
    def _():
        corner_gather.start()
    for m in range(5):
        mask_tiles(m)
    ag_step(1, 0)
    mask_tiles(5)
    mask_tiles(6)
    x_lo_copy(False).wait_recv()
    for j in (2, 1, 3):
        start(row_copy(j, 0, True))
    start(remote(own, own, hp_s, hp_r, hpartner))
    ag_step(1, 1)
    mask_tiles(7)
    ts[...] = am[r, opposite[1]]
    tile_copy = remote(ts, tr, tt_s, tt_r, opposite)
    start(tile_copy)
    ag_step(2, 0)
    ag_step(1, 2)
    ag_step(2, 1)
    other = ht.at[block(0, 0, q)]
    remote(other, other, hp_s, hp_r, hpartner).wait_recv()
    share(0, 0)
    ag_step(3, 0)
    ag_step(2, 2)
    share_wait(0)
    back_pass((2, 1, 3, 0), (0,), True)
    ag_step(3, 1)
    share_wait(1, 7)
    back_pass((2, 1), (1, 7), False)
    for j in (2, 1, 3):
        for same in (1, 0):
            row_copy(j, same, False).wait_recv()

    def rows_of(k):
        return jnp.concatenate([am[m, k] for m in range(NM)], axis=1)

    def product(ds, qq):
        lhs = jnp.concatenate([rows_of(block(d, hh, qq)) for d in ds for hh in range(2)], axis=0)
        out = jnp.dot(lhs, nat[...].reshape(NM * TILE, F), preferred_element_type=jnp.float32)
        return out.reshape(len(ds), 2, TILE, F)

    def dd(d, hh):
        return remote(snd.at[d, hh], sib.at[d, hh], dd_s.at[d, hh], dd_r.at[d, hh], sibling)

    def forward(ds):
        out = product(ds, 1 - q)
        for i, d in enumerate(ds):
            snd[d] = out[i]
            start(dd(d, 0))
        for d in ds:
            start(dd(d, 1))
        out = product(ds, q)
        for i, d in enumerate(ds):
            keep[d] = out[i]

    def xx(d):
        return remote(xs.at[d], xr.at[d], xx_s.at[d], xx_r.at[d], hpartner)

    def cross_sums(d):
        dd(d, 0).wait_recv()
        xs[d] = (keep[d, 0, :, HALF:] + sib[d, 0, :, HALF:]).astype(jnp.bfloat16)
        start(xx(d))

    def rs_rows(p):
        return (0, TILE) if p == 0 else (64 * (p - 1), 64)

    def rsz(dirn, s, p):
        src, dst = (cs0, cr0) if p == 0 else (cs1, cr1)
        part = pl.ds(*rs_rows(p))
        return remote(src.at[dirn, s - 1].at[part], dst.at[dirn, s - 1].at[part],
                      rsz_s.at[dirn, s - 1, p], rsz_r.at[dirn, s - 1, p], zdev[dirn])

    def rs_step(s, p):
        out, got = (cs0, cr0) if p == 0 else (cs1, cr1)
        hh = 0 if p == 0 else 1
        lo, size = rs_rows(p)
        rows = slice(lo, lo + size)
        for dirn in range(2):
            d = 5 - s if dirn == 0 else 3 + s
            if p == 1:
                dd(d, 1).wait_recv()
                xx(d).wait_recv()
            if s > 2:
                rsz(dirn, s - 1, p).wait_recv()

            def sums(cols, extra):
                value = keep[d, hh, rows, cols] + sib[d, hh, rows, cols]
                if extra is not None:
                    value = value + extra.astype(jnp.float32)
                if s > 2:
                    value = value + got[dirn, s - 2, rows, cols].astype(jnp.float32)
                out[dirn, s - 1, rows, cols] = value.astype(jnp.bfloat16)
            sums(slice(0, HALF), None)
            if hh == 1:
                sums(slice(HALF, F), xr[d, rows])
            start(rsz(dirn, s, p))

    def brow(j, same, sending=True):
        dev = (row_at(j if sending else -j, same), c)
        return remote(bs.at[j, same], br.at[j, same], br_s.at[j, same], br_r.at[j, same], dev)

    def backward(j):
        back_pass((j,), (2, 6, 3, 5, 4), False)
        for same in range(2):
            bs[j, same] = acc[j, :, TILE * same:TILE * (same + 1)].astype(jnp.bfloat16)
            if j or not same:
                start(brow(j, same))

    corner_sums = remote(ns, nr, cn_s, cn_r, corner)

    def corner_product():
        @pl.when(at_corner)
        def _():
            ns[...] = jnp.dot(rows_of(corner[1]), nat[...].reshape(NM * TILE, F),
                              preferred_element_type=jnp.float32).astype(jnp.bfloat16)
            corner_sums.start()

    forward((3, 5))
    back_pass((3, 0), (1, 7), False)
    forward((2, 6))
    ag_step(3, 2)
    for p in range(2):
        ag_step(4, p)
    cross_sums(3)
    cross_sums(5)
    rs_step(2, 0)
    forward((1, 7))
    corner_product()
    share_wait(2, 6, 3, 5)

    @pl.when(at_corner)
    def _():
        corner_gather.wait_recv()
    backward(2)
    cross_sums(2)
    cross_sums(6)
    rs_step(2, 1)
    rs_step(2, 2)
    backward(1)
    cross_sums(1)
    cross_sums(7)
    rs_step(3, 0)
    backward(3)
    rs_step(3, 1)
    rs_step(3, 2)
    backward(0)
    forward((0,))
    rs_step(4, 0)
    cross_sums(0)
    rs_step(4, 1)
    rs_step(4, 2)

    back = acc[0, :, TILE:]
    tile_copy.wait_recv()
    back = back + lax.dot_general(ht[opposite[1]], tr[...], (((1,), (1,)), ((), ())),
                                  preferred_element_type=jnp.float32)
    for j in (2, 1, 3, 0):
        for same in range(2):
            if j or not same:
                brow(j, same, False).wait_recv()
                back = back + br[j, same].astype(jnp.float32)
    dd(0, 1).wait_recv()
    keep[0, 1] = keep[0, 1] + sib[0, 1] + back.T

    @pl.when(at_corner)
    def _():
        corner_sums.wait_recv()
        keep[0, 1] = keep[0, 1] + nr[...].astype(jnp.float32)
    for dirn in range(2):
        rsz(dirn, 4, 0).wait_recv()
    near = slice(0, HALF)
    hs[...] = (keep[0, 0, :, near] + sib[0, 0, :, near] + cr0[0, 3].astype(jnp.float32)
               + cr0[1, 3].astype(jnp.float32)).astype(jnp.bfloat16)
    cross = remote(hs, hr, hx_s, hx_r, hpartner)
    start(cross)
    xx(0).wait_recv()
    for p in (1, 2):
        for dirn in range(2):
            rsz(dirn, 4, p).wait_recv()
    summed = keep[0, 1] + cr1[0, 3].astype(jnp.float32) + cr1[1, 3].astype(jnp.float32)
    cross.wait_recv()
    summed = summed + jnp.concatenate([hr[...], xr[0]], axis=1).astype(jnp.float32)
    mixed = jnp.dot(summed, p_ref[...], precision=lax.Precision.HIGHEST,
                    preferred_element_type=jnp.float32)
    lifted = x_ref[...] + jnp.maximum(mixed, 0.0)
    scale = lax.rsqrt(jnp.mean(lifted * lifted, axis=-1, keepdims=True) + 1e-06)
    o_ref[...] = lifted * scale * g_ref[...]
    for copy in sends:
        copy.wait_send()

    @pl.when(at_corner)
    def _():
        corner_gather.wait_send()
        corner_sums.wait_send()


def shards(features, adjacency, tile_mask, projection, row_gain):
    vm = pl.BlockSpec(memory_space=pltpu.VMEM)
    bf, f32 = jnp.bfloat16, jnp.float32
    dma = pltpu.SemaphoreType.DMA
    out = pl.pallas_call(
        kernel,
        out_shape=jax.ShapeDtypeStruct((TILE, F), f32),
        in_specs=[vm, pl.BlockSpec(memory_space=pl.ANY),
                  pl.BlockSpec(memory_space=pltpu.SMEM), vm, vm],
        out_specs=vm,
        scratch_shapes=[
            pltpu.VMEM((NM, NK, TILE, TILE), bf),
            pltpu.VMEM((8, TILE, F), bf),
            pltpu.VMEM((NK, F, TILE), bf),
            pltpu.VMEM((8, 2, TILE, F), f32),
            pltpu.VMEM((8, 2, TILE, F), f32),
            pltpu.VMEM((8, 2, TILE, F), f32),
            pltpu.VMEM((2, 4, TILE, HALF), bf),
            pltpu.VMEM((2, 4, TILE, HALF), bf),
            pltpu.VMEM((2, 4, TILE, F), bf),
            pltpu.VMEM((2, 4, TILE, F), bf),
            pltpu.VMEM((8, TILE, F - HALF), bf),
            pltpu.VMEM((8, TILE, F - HALF), bf),
            pltpu.VMEM((TILE, HALF), bf),
            pltpu.VMEM((TILE, HALF), bf),
            pltpu.VMEM((4, F, 2 * TILE), f32),
            pltpu.VMEM((4, 2, F, TILE), bf),
            pltpu.VMEM((4, 2, F, TILE), bf),
            pltpu.VMEM((TILE, TILE), bf),
            pltpu.VMEM((TILE, TILE), bf),
            pltpu.VMEM((TILE, F), bf),
            pltpu.VMEM((TILE, F), bf),
            dma((NM,)), dma((4, 2)), dma((4, 2)), dma, dma, dma((2, 4, 3)), dma((2, 4, 3)),
            dma, dma, dma((8,)), dma((8,)), dma((8, 2)), dma((8, 2)),
            dma((8, 2)), dma((8, 2)), dma((8,)), dma((8,)), dma((2, 4, 3)), dma((2, 4, 3)),
            dma, dma, dma((4, 2)), dma((4, 2)), dma, dma, dma, dma, dma, dma,
        ],
        compiler_params=pltpu.CompilerParams(
            collective_id=0, has_side_effects=True, vmem_limit_bytes=56 * 2**20),
        cost_estimate=pl.CostEstimate(
            flops=4 * 32 * 1024 * 128 * 512, bytes_accessed=9 * 2**20, transcendentals=128),
    )(features[0, 0], adjacency[:, 0, 0], tile_mask[:, 0, 0].T, projection[0], row_gain)
    return out[None, None]


def solution(mesh):
    return jax.shard_map(
        shards,
        mesh=mesh,
        in_specs=(
            P("col", "row", None, None),
            P(None, "row", "col", None, None, None),
            P(None, "row", "col", None),
            P(),
            P(),
        ),
        out_specs=P("col", "row", None, None),
        check_vma=False,
    )
```

```python
import functools

import jax
import jax.numpy as jnp
from jax import lax
from jax.experimental import pallas as pl
from jax.experimental.pallas import tpu as pltpu
from jax.sharding import PartitionSpec as P

MESH = pl.DeviceIdType.MESH
TILE, F, NK, NM, NZ = 128, 512, 32, 8, 8
HALF = 256


def kernel(x_ref, a_hbm, mask_ref, p_ref, g_ref, o_ref,
           am, nat, ht, keep, snd, sib, cs0, cr0, cs1, cr1, xs, xr, hs, hr, acc, bs, br, ls, lr, ts, tr,
           ns, nr, fs, lo_s, lo_r, a_sem, row_s, row_r, xl_s, xl_r, agz_s, agz_r, hp_s, hp_r, xg_s, xg_r, sh_s, sh_r,
           dd_s, dd_r, xx_s, xx_r, rsz_s, rsz_r, hx_s, hx_r, br_s, br_r, tt_s, tt_r,
           cg_s, cg_r, cn_s, cn_r):
    r = lax.axis_index("row")
    c = lax.axis_index("col")
    xl, y = r // 4, r % 4
    z = c // 4
    h = (c // 2) % 2
    q = c % 2
    sibling = (r, c + 1 - 2 * q)
    hpartner = (r, c + 2 - 4 * h)
    lpartner = ((r + 4) % 8, c)
    zdev = ((r, (c + 4) % NK), (r, (c + 28) % NK))

    def row_at(j, same):
        return 4 * (xl if same else 1 - xl) + (y + j + 4) % 4

    def plane(d):
        return (z + d + 16) % NZ

    def block(d, hh, qq):
        return 4 * plane(d) + 2 * (h if hh == 1 else 1 - h) + qq

    opposite = (r, block(4, 1, q))
    corner = (r, block(4, 0, 1 - q))
    at_corner = jnp.logical_and(h == q, jnp.logical_or(
        jnp.logical_and(h == 1, z < 4), jnp.logical_and(h == 0, z >= 4)))
    zdiag = tuple((r, block(d, 0, q)) for d in (1, -1))

    sends = []

    def remote(src, dst, ssem, rsem, dev):
        return pltpu.make_async_remote_copy(
            src_ref=src, dst_ref=dst, send_sem=ssem, recv_sem=rsem,
            device_id=dev, device_id_type=MESH)

    def start(copy):
        copy.start()
        sends.append(copy)

    for m in range(NM):
        pltpu.make_async_copy(a_hbm.at[:, m], am.at[m], a_sem.at[m]).start()

    barrier = pltpu.get_barrier_semaphore()
    peers = ([(row_at(j, 1), c) for j in range(1, 4)]
             + [lpartner, sibling, hpartner, (r, block(0, 0, 1 - q)), *zdev, *zdiag])
    for dev in peers:
        pl.semaphore_signal(barrier, inc=1, device_id=dev, device_id_type=MESH)

    x = x_ref[...]
    nat[r] = x.astype(jnp.bfloat16)
    ht[c] = x.T.astype(jnp.bfloat16)
    pl.semaphore_wait(barrier, len(peers))

    @pl.when(jnp.logical_not(at_corner))
    def _():
        ht[corner[1]] = jnp.zeros((F, TILE), jnp.bfloat16)

    def ag_ways(s, p):
        return (0, 1) if s < 4 else ((1,), (0,), ())[p]

    def ag_copy(dirn, s, p, sending):
        d = (1 - s if sending else -s) if dirn == 0 else (s - 1 if sending else s)
        lo, size = (HALF, HALF) if p == 0 else (0, HALF)
        hh, dev = (0 if p == 2 else 1), zdev[dirn]
        if p == 2 and s == 1 and sending:
            hh, dev = 1, zdiag[dirn]
        ref = ht.at[block(d, hh, q)].at[pl.ds(lo, size)]
        return remote(ref, ref, agz_s.at[dirn, s - 1, p], agz_r.at[dirn, s - 1, p], dev)

    def ag_send(s, p):
        for dirn in ag_ways(s, p):
            start(ag_copy(dirn, s, p, True))

    def cross_gather(d, hh):
        ref = ht.at[block(d, hh, q)].at[pl.ds(HALF, F - HALF)]
        return remote(ref, ref, xg_s.at[d], xg_r.at[d], hpartner)

    def share(d, hh):
        ref = ht.at[block(d, hh, q)]
        start(remote(ref, ref, sh_s.at[d, hh], sh_r.at[d, hh], sibling))

    def share_wait(*ds):
        for d in ds:
            for hh in (1, 0):
                ref = ht.at[block(d, hh, 1 - q)]
                remote(ref, ref, sh_s.at[d, hh], sh_r.at[d, hh], sibling).wait_recv()

    def ag_step(s, p):
        for dirn in ag_ways(s, p):
            ag_copy(dirn, s, p, False).wait_recv()
            if s < 4 and dirn in ag_ways(s + 1, p):
                start(ag_copy(dirn, s + 1, p, True))
        for d in ((8 - s, s) if s < 4 else ()):
            if p == 0:
                start(cross_gather(d, 1))
            elif p == 1:
                share(d, 1)
            else:
                cross_gather(d, 0).wait_recv()
                share(d, 0)

    def row_copy(j, same, sending):
        ref = nat.at[row_at(0, same) if sending else row_at(-j, same)]
        return remote(ref, ref, row_s.at[j, same], row_r.at[j, same], (row_at(j, 1), c))

    def x_lo_copy(sending):
        ref = nat.at[r if sending else (r + 4) % 8]
        return remote(ref, ref, xl_s, xl_r, lpartner)

    def mask_tiles(m):
        pltpu.make_async_copy(a_hbm.at[:, m], am.at[m], a_sem.at[m]).wait()

        def body(k, carry):
            level = jnp.full((TILE, TILE), mask_ref[m, k].astype(jnp.float32))
            am[m, k] = am[m, k] * level.astype(jnp.bfloat16)
            return carry
        lax.fori_loop(0, NK, body, 0)

    def back_pass(js, ds, first):
        ks = [block(d, hh, qq) for d in ds for hh in range(2) for qq in (q, 1 - q)
              if d != 4 or (hh, qq is q) in ((1, True), (0, False))]
        for j in js:
            lhs = jnp.concatenate([ht[k] for k in ks], axis=1)
            rhs = jnp.concatenate(
                [jnp.concatenate([am[row_at(j, same), k] for k in ks], axis=0)
                 for same in range(2)], axis=1)
            term = jnp.dot(lhs, rhs, preferred_element_type=jnp.float32)
            acc[j] = term if first else acc[j] + term

    own = ht.at[c]
    start(x_lo_copy(True))
    for j in (2, 1, 3):
        start(row_copy(j, 1, True))
    for p in range(3):
        ag_send(1, p)
    share(0, 1)
    corner_gather = remote(own, own, cg_s, cg_r, corner)

    def far_signal(i):
        for dev in zdev:
            pl.semaphore_signal(fs.at[i], inc=1, device_id=dev, device_id_type=MESH)

    def far_wait(i):
        pl.semaphore_wait(fs.at[i], 2)

    far_signal(0)
    for m in range(5):
        mask_tiles(m)
        if m % 2 == 1:
            far_wait(m // 2)
            far_signal(m // 2 + 1)
    ag_step(1, 0)
    far_wait(2)
    far_signal(3)
    mask_tiles(5)
    mask_tiles(6)
    x_lo_copy(False).wait_recv()
    for j in (2, 1, 3):
        start(row_copy(j, 0, True))
    start(remote(own, own, hp_s, hp_r, hpartner))
    ag_step(1, 1)
    mask_tiles(7)
    far_wait(3)

    @pl.when(at_corner)
    def _():
        corner_gather.start()
    ts[...] = am[r, opposite[1]]
    tile_copy = remote(ts, tr, tt_s, tt_r, opposite)
    start(tile_copy)
    ag_step(2, 0)
    ag_step(1, 2)
    ag_step(2, 1)
    other = ht.at[block(0, 0, q)]
    remote(other, other, hp_s, hp_r, hpartner).wait_recv()
    share(0, 0)
    ag_step(3, 0)
    ag_step(2, 2)
    share_wait(0)
    back_pass((2, 1, 3, 0), (0,), True)
    ag_step(3, 1)
    share_wait(1, 7)
    back_pass((2, 1), (1, 7), False)
    for j in (2, 1, 3):
        for same in (1, 0):
            row_copy(j, same, False).wait_recv()

    def rows_of(k):
        return jnp.concatenate([am[m, k] for m in range(NM)], axis=1)

    def product(ds, qq):
        lhs = jnp.concatenate([rows_of(block(d, hh, qq)) for d in ds for hh in range(2)], axis=0)
        out = jnp.dot(lhs, nat[...].reshape(NM * TILE, F), preferred_element_type=jnp.float32)
        return out.reshape(len(ds), 2, TILE, F)

    def dd(d, hh):
        return remote(snd.at[d, hh], sib.at[d, hh], dd_s.at[d, hh], dd_r.at[d, hh], sibling)

    def forward(ds):
        out = product(ds, 1 - q)
        for i, d in enumerate(ds):
            snd[d] = out[i]
            start(dd(d, 0))
        for d in ds:
            start(dd(d, 1))
        out = product(ds, q)
        for i, d in enumerate(ds):
            keep[d] = out[i]

    def xx(d):
        return remote(xs.at[d], xr.at[d], xx_s.at[d], xx_r.at[d], hpartner)

    def cross_sums(d):
        dd(d, 0).wait_recv()
        xs[d] = (keep[d, 0, :, HALF:] + sib[d, 0, :, HALF:]).astype(jnp.bfloat16)
        start(xx(d))

    def rs_rows(p):
        return (0, TILE) if p == 0 else (64 * (p - 1), 64)

    def rsz(dirn, s, p):
        src, dst = (cs0, cr0) if p == 0 else (cs1, cr1)
        part = pl.ds(*rs_rows(p))
        return remote(src.at[dirn, s - 1].at[part], dst.at[dirn, s - 1].at[part],
                      rsz_s.at[dirn, s - 1, p], rsz_r.at[dirn, s - 1, p], zdev[dirn])

    def rs_step(s, p):
        out, got = (cs0, cr0) if p == 0 else (cs1, cr1)
        hh = 0 if p == 0 else 1
        lo, size = rs_rows(p)
        rows = slice(lo, lo + size)
        for dirn in range(2):
            d = 5 - s if dirn == 0 else 3 + s
            if p == 1:
                dd(d, 1).wait_recv()
                xx(d).wait_recv()
            if s > 2:
                rsz(dirn, s - 1, p).wait_recv()

            def sums(cols, extra):
                value = keep[d, hh, rows, cols] + sib[d, hh, rows, cols]
                if extra is not None:
                    value = value + extra.astype(jnp.float32)
                if s > 2:
                    value = value + got[dirn, s - 2, rows, cols].astype(jnp.float32)
                out[dirn, s - 1, rows, cols] = value.astype(jnp.bfloat16)
            sums(slice(0, HALF), None)
            if hh == 1:
                sums(slice(HALF, F), xr[d, rows])
            start(rsz(dirn, s, p))

    def brow(j, same):
        return remote(bs.at[j, same], br.at[j, same], br_s.at[j, same], br_r.at[j, same],
                      (row_at(j, 1), c))

    def backward(j):
        back_pass((j,), (2, 6, 3, 5, 4), False)
        for same in range(2):
            bs[j, same] = acc[j, :, TILE * same:TILE * (same + 1)].astype(jnp.bfloat16)
            if j:
                start(brow(j, same))

    corner_sums = remote(ns, nr, cn_s, cn_r, corner)

    def corner_product():
        @pl.when(at_corner)
        def _():
            ns[...] = jnp.dot(rows_of(corner[1]), nat[...].reshape(NM * TILE, F),
                              preferred_element_type=jnp.float32).astype(jnp.bfloat16)
            corner_sums.start()

    forward((3, 5))
    back_pass((3, 0), (1, 7), False)
    forward((2, 6))
    ag_step(3, 2)
    for p in range(2):
        ag_step(4, p)
    cross_sums(3)
    cross_sums(5)
    rs_step(2, 0)
    forward((1, 7))
    corner_product()
    share_wait(2, 6, 3, 5)

    @pl.when(at_corner)
    def _():
        corner_gather.wait_recv()
    backward(2)
    cross_sums(2)
    cross_sums(6)
    rs_step(2, 1)
    rs_step(2, 2)
    backward(1)
    cross_sums(1)
    cross_sums(7)
    rs_step(3, 0)
    backward(3)
    rs_step(3, 1)
    rs_step(3, 2)
    backward(0)
    forward((0,))
    rs_step(4, 0)
    cross_sums(0)
    rs_step(4, 1)
    rs_step(4, 2)

    def back_sum(same):
        value = acc[0, :, TILE * same:TILE * (same + 1)]
        for j in (1, 3, 2):
            brow(j, same).wait_recv()
            value = value + br[j, same].astype(jnp.float32)
        return value

    ls[...] = back_sum(0).astype(jnp.bfloat16)
    across = remote(ls, lr, lo_s, lo_r, lpartner)
    start(across)
    tile_copy.wait_recv()
    back = back_sum(1) + lax.dot_general(ht[opposite[1]], tr[...], (((1,), (1,)), ((), ())),
                                         preferred_element_type=jnp.float32)
    dd(0, 1).wait_recv()
    keep[0, 1] = keep[0, 1] + sib[0, 1]

    @pl.when(at_corner)
    def _():
        corner_sums.wait_recv()
        keep[0, 1] = keep[0, 1] + nr[...].astype(jnp.float32)
    for dirn in range(2):
        rsz(dirn, 4, 0).wait_recv()
    near = slice(0, HALF)
    hs[...] = (keep[0, 0, :, near] + sib[0, 0, :, near] + cr0[0, 3].astype(jnp.float32)
               + cr0[1, 3].astype(jnp.float32)).astype(jnp.bfloat16)
    cross = remote(hs, hr, hx_s, hx_r, hpartner)
    start(cross)
    across.wait_recv()
    keep[0, 1] = keep[0, 1] + (back + lr[...].astype(jnp.float32)).T
    xx(0).wait_recv()
    for p in (1, 2):
        for dirn in range(2):
            rsz(dirn, 4, p).wait_recv()
    summed = keep[0, 1] + cr1[0, 3].astype(jnp.float32) + cr1[1, 3].astype(jnp.float32)
    cross.wait_recv()
    summed = summed + jnp.concatenate([hr[...], xr[0]], axis=1).astype(jnp.float32)
    mixed = jnp.dot(summed, p_ref[...], precision=lax.Precision.HIGHEST,
                    preferred_element_type=jnp.float32)
    lifted = x_ref[...] + jnp.maximum(mixed, 0.0)
    scale = lax.rsqrt(jnp.mean(lifted * lifted, axis=-1, keepdims=True) + 1e-06)
    o_ref[...] = lifted * scale * g_ref[...]
    for copy in sends:
        copy.wait_send()

    @pl.when(at_corner)
    def _():
        corner_gather.wait_send()
        corner_sums.wait_send()


def shards(features, adjacency, tile_mask, projection, row_gain):
    vm = pl.BlockSpec(memory_space=pltpu.VMEM)
    bf, f32 = jnp.bfloat16, jnp.float32
    dma = pltpu.SemaphoreType.DMA
    out = pl.pallas_call(
        kernel,
        out_shape=jax.ShapeDtypeStruct((TILE, F), f32),
        in_specs=[vm, pl.BlockSpec(memory_space=pl.ANY),
                  pl.BlockSpec(memory_space=pltpu.SMEM), vm, vm],
        out_specs=vm,
        scratch_shapes=[
            pltpu.VMEM((NM, NK, TILE, TILE), bf),
            pltpu.VMEM((8, TILE, F), bf),
            pltpu.VMEM((NK, F, TILE), bf),
            pltpu.VMEM((8, 2, TILE, F), f32),
            pltpu.VMEM((8, 2, TILE, F), f32),
            pltpu.VMEM((8, 2, TILE, F), f32),
            pltpu.VMEM((2, 4, TILE, HALF), bf),
            pltpu.VMEM((2, 4, TILE, HALF), bf),
            pltpu.VMEM((2, 4, TILE, F), bf),
            pltpu.VMEM((2, 4, TILE, F), bf),
            pltpu.VMEM((8, TILE, F - HALF), bf),
            pltpu.VMEM((8, TILE, F - HALF), bf),
            pltpu.VMEM((TILE, HALF), bf),
            pltpu.VMEM((TILE, HALF), bf),
            pltpu.VMEM((4, F, 2 * TILE), f32),
            pltpu.VMEM((4, 2, F, TILE), bf),
            pltpu.VMEM((4, 2, F, TILE), bf),
            pltpu.VMEM((F, TILE), bf),
            pltpu.VMEM((F, TILE), bf),
            pltpu.VMEM((TILE, TILE), bf),
            pltpu.VMEM((TILE, TILE), bf),
            pltpu.VMEM((TILE, F), bf),
            pltpu.VMEM((TILE, F), bf),
            pltpu.SemaphoreType.REGULAR((4,)), dma, dma,
            dma((NM,)), dma((4, 2)), dma((4, 2)), dma, dma, dma((2, 4, 3)), dma((2, 4, 3)),
            dma, dma, dma((8,)), dma((8,)), dma((8, 2)), dma((8, 2)),
            dma((8, 2)), dma((8, 2)), dma((8,)), dma((8,)), dma((2, 4, 3)), dma((2, 4, 3)),
            dma, dma, dma((4, 2)), dma((4, 2)), dma, dma, dma, dma, dma, dma,
        ],
        compiler_params=pltpu.CompilerParams(
            collective_id=0, has_side_effects=True, vmem_limit_bytes=56 * 2**20),
        cost_estimate=pl.CostEstimate(
            flops=4 * 32 * 1024 * 128 * 512, bytes_accessed=9 * 2**20, transcendentals=128),
    )(features[0, 0], adjacency[:, 0, 0], tile_mask[:, 0, 0].T, projection[0], row_gain)
    return out[None, None]


def solution(mesh):
    return jax.shard_map(
        shards,
        mesh=mesh,
        in_specs=(
            P("col", "row", None, None),
            P(None, "row", "col", None, None, None),
            P(None, "row", "col", None),
            P(),
            P(),
        ),
        out_specs=P("col", "row", None, None),
        check_vma=False,
    )
```

```python
import functools

import jax
import jax.numpy as jnp
from jax import lax
from jax.experimental import pallas as pl
from jax.experimental.pallas import tpu as pltpu
from jax.sharding import PartitionSpec as P

MESH = pl.DeviceIdType.MESH
TILE, F, NK, NM, NZ = 128, 512, 32, 8, 8
HALF = 256


def kernel(x_ref, a_hbm, mask_ref, p_ref, g_ref, o_ref,
           am, nat, ht, keep, snd, sib, cs0, cr0, cs1, cr1, xs, xr, hs, hr, acc, bs, br, ls, lr, ts, tr,
           ns, nr, fs, lo_s, lo_r, a_sem, row_s, row_r, xl_s, xl_r, agz_s, agz_r, hp_s, hp_r, xg_s, xg_r, sh_s, sh_r,
           dd_s, dd_r, xx_s, xx_r, rsz_s, rsz_r, hx_s, hx_r, br_s, br_r, tt_s, tt_r,
           cg_s, cg_r, cn_s, cn_r):
    r = lax.axis_index("row")
    c = lax.axis_index("col")
    xl, y = r // 4, r % 4
    z = c // 4
    h = (c // 2) % 2
    q = c % 2
    sibling = (r, c + 1 - 2 * q)
    hpartner = (r, c + 2 - 4 * h)
    lpartner = ((r + 4) % 8, c)
    zdev = ((r, (c + 4) % NK), (r, (c + 28) % NK))

    def row_at(j, same):
        return 4 * (xl if same else 1 - xl) + (y + j + 4) % 4

    def plane(d):
        return (z + d + 16) % NZ

    def block(d, hh, qq):
        return 4 * plane(d) + 2 * (h if hh == 1 else 1 - h) + qq

    opposite = (r, block(4, 1, q))
    corner = (r, block(4, 0, 1 - q))
    at_corner = jnp.logical_and(h == q, jnp.logical_or(
        jnp.logical_and(h == 1, z < 4), jnp.logical_and(h == 0, z >= 4)))
    zdiag = tuple((r, block(d, 0, q)) for d in (1, -1))

    sends = []

    def remote(src, dst, ssem, rsem, dev):
        return pltpu.make_async_remote_copy(
            src_ref=src, dst_ref=dst, send_sem=ssem, recv_sem=rsem,
            device_id=dev, device_id_type=MESH)

    def start(copy):
        copy.start()
        sends.append(copy)

    for m in range(NM):
        pltpu.make_async_copy(a_hbm.at[:, m], am.at[m], a_sem.at[m]).start()

    barrier = pltpu.get_barrier_semaphore()
    peers = ([(row_at(j, 1), c) for j in range(1, 4)]
             + [lpartner, sibling, hpartner, (r, block(0, 0, 1 - q)), *zdev, *zdiag])
    for dev in peers:
        pl.semaphore_signal(barrier, inc=1, device_id=dev, device_id_type=MESH)

    x = x_ref[...]
    nat[r] = x.astype(jnp.bfloat16)
    ht[c] = x.T.astype(jnp.bfloat16)
    pl.semaphore_wait(barrier, len(peers))

    @pl.when(jnp.logical_not(at_corner))
    def _():
        ht[corner[1]] = jnp.zeros((F, TILE), jnp.bfloat16)

    def ag_ways(s, p):
        return (0, 1) if s < 4 else ((1,), (0,), ())[p]

    def ag_copy(dirn, s, p, sending):
        d = (1 - s if sending else -s) if dirn == 0 else (s - 1 if sending else s)
        lo, size = (HALF, HALF) if p == 0 else (0, HALF)
        hh, dev = (0 if p == 2 else 1), zdev[dirn]
        if p == 2 and s == 1 and sending:
            hh, dev = 1, zdiag[dirn]
        ref = ht.at[block(d, hh, q)].at[pl.ds(lo, size)]
        return remote(ref, ref, agz_s.at[dirn, s - 1, p], agz_r.at[dirn, s - 1, p], dev)

    def ag_send(s, p):
        for dirn in ag_ways(s, p):
            start(ag_copy(dirn, s, p, True))

    def cross_gather(d, hh):
        ref = ht.at[block(d, hh, q)].at[pl.ds(HALF, F - HALF)]
        return remote(ref, ref, xg_s.at[d], xg_r.at[d], hpartner)

    def share(d, hh):
        ref = ht.at[block(d, hh, q)]
        start(remote(ref, ref, sh_s.at[d, hh], sh_r.at[d, hh], sibling))

    def share_wait(*ds):
        for d in ds:
            for hh in (1, 0):
                ref = ht.at[block(d, hh, 1 - q)]
                remote(ref, ref, sh_s.at[d, hh], sh_r.at[d, hh], sibling).wait_recv()

    def ag_step(s, p):
        for dirn in ag_ways(s, p):
            ag_copy(dirn, s, p, False).wait_recv()
            if s < 4 and dirn in ag_ways(s + 1, p):
                start(ag_copy(dirn, s + 1, p, True))
        for d in ((8 - s, s) if s < 4 else ()):
            if p == 0:
                start(cross_gather(d, 1))
            elif p == 1:
                share(d, 1)
            else:
                cross_gather(d, 0).wait_recv()
                share(d, 0)

    def row_copy(j, same, sending):
        ref = nat.at[row_at(0, same) if sending else row_at(-j, same)]
        return remote(ref, ref, row_s.at[j, same], row_r.at[j, same], (row_at(j, 1), c))

    def x_lo_copy(sending):
        ref = nat.at[r if sending else (r + 4) % 8]
        return remote(ref, ref, xl_s, xl_r, lpartner)

    def mask_tiles(m):
        pltpu.make_async_copy(a_hbm.at[:, m], am.at[m], a_sem.at[m]).wait()

        def body(k, carry):
            level = jnp.full((TILE, TILE), mask_ref[m, k].astype(jnp.float32))
            am[m, k] = am[m, k] * level.astype(jnp.bfloat16)
            return carry
        lax.fori_loop(0, NK, body, 0)

    def back_pass(js, ds, first):
        ks = [block(d, hh, qq) for d in ds for hh in range(2) for qq in (q, 1 - q)
              if d != 4 or (hh, qq is q) in ((1, True), (0, False))]
        for j in js:
            lhs = jnp.concatenate([ht[k] for k in ks], axis=1)
            rhs = jnp.concatenate(
                [jnp.concatenate([am[row_at(j, same), k] for k in ks], axis=0)
                 for same in range(2)], axis=1)
            term = jnp.dot(lhs, rhs, preferred_element_type=jnp.float32)
            acc[j] = term if first else acc[j] + term

    own = ht.at[c]
    start(x_lo_copy(True))
    for j in (2, 1, 3):
        start(row_copy(j, 1, True))
    for p in range(3):
        ag_send(1, p)
    share(0, 1)
    corner_gather = remote(own, own, cg_s, cg_r, corner)

    def far_signal(i):
        for dev in zdev:
            pl.semaphore_signal(fs.at[i], inc=1, device_id=dev, device_id_type=MESH)

    def far_wait(i):
        pl.semaphore_wait(fs.at[i], 2)

    far_signal(0)
    for m in range(5):
        mask_tiles(m)
        if m % 2 == 1:
            far_wait(m // 2)
            far_signal(m // 2 + 1)
    ag_step(1, 0)
    far_wait(2)
    far_signal(3)
    mask_tiles(5)
    mask_tiles(6)
    x_lo_copy(False).wait_recv()
    for j in (2, 1, 3):
        start(row_copy(j, 0, True))
    start(remote(own, own, hp_s, hp_r, hpartner))
    ag_step(1, 1)
    mask_tiles(7)
    far_wait(3)

    @pl.when(at_corner)
    def _():
        corner_gather.start()
    ts[...] = am[r, opposite[1]]
    tile_copy = remote(ts, tr, tt_s, tt_r, opposite)
    start(tile_copy)
    ag_step(2, 0)
    ag_step(1, 2)
    ag_step(2, 1)
    other = ht.at[block(0, 0, q)]
    remote(other, other, hp_s, hp_r, hpartner).wait_recv()
    share(0, 0)
    ag_step(3, 0)
    ag_step(2, 2)
    share_wait(0)
    back_pass((2, 1, 3, 0), (0,), True)
    ag_step(3, 1)
    share_wait(1, 7)
    back_pass((2, 1), (1, 7), False)
    for j in (2, 1, 3):
        for same in (1, 0):
            row_copy(j, same, False).wait_recv()

    def rows_of(k):
        return jnp.concatenate([am[m, k] for m in range(NM)], axis=1)

    def product(ds, qq):
        lhs = jnp.concatenate([rows_of(block(d, hh, qq)) for d in ds for hh in range(2)], axis=0)
        out = jnp.dot(lhs, nat[...].reshape(NM * TILE, F), preferred_element_type=jnp.float32)
        return out.reshape(len(ds), 2, TILE, F)

    def dd(d, hh):
        return remote(snd.at[d, hh], sib.at[d, hh], dd_s.at[d, hh], dd_r.at[d, hh], sibling)

    def forward(ds):
        out = product(ds, 1 - q)
        for i, d in enumerate(ds):
            snd[d] = out[i]
            start(dd(d, 0))
        for d in ds:
            start(dd(d, 1))
        out = product(ds, q)
        for i, d in enumerate(ds):
            keep[d] = out[i]

    def xx(d):
        return remote(xs.at[d], xr.at[d], xx_s.at[d], xx_r.at[d], hpartner)

    def cross_sums(d):
        dd(d, 0).wait_recv()
        xs[d] = (keep[d, 0, :, HALF:] + sib[d, 0, :, HALF:]).astype(jnp.bfloat16)
        start(xx(d))

    def rs_rows(p):
        return (0, TILE) if p == 0 else (64 * (p - 1), 64)

    def rsz(dirn, s, p):
        src, dst = (cs0, cr0) if p == 0 else (cs1, cr1)
        part = pl.ds(*rs_rows(p))
        return remote(src.at[dirn, s - 1].at[part], dst.at[dirn, s - 1].at[part],
                      rsz_s.at[dirn, s - 1, p], rsz_r.at[dirn, s - 1, p], zdev[dirn])

    def rs_step(s, p):
        out, got = (cs0, cr0) if p == 0 else (cs1, cr1)
        hh = 0 if p == 0 else 1
        lo, size = rs_rows(p)
        rows = slice(lo, lo + size)
        for dirn in range(2):
            d = 5 - s if dirn == 0 else 3 + s
            if p == 1:
                dd(d, 1).wait_recv()
                xx(d).wait_recv()
            if s > 2:
                rsz(dirn, s - 1, p).wait_recv()

            def sums(cols, extra):
                value = keep[d, hh, rows, cols] + sib[d, hh, rows, cols]
                if extra is not None:
                    value = value + extra.astype(jnp.float32)
                if s > 2:
                    value = value + got[dirn, s - 2, rows, cols].astype(jnp.float32)
                out[dirn, s - 1, rows, cols] = value.astype(jnp.bfloat16)
            sums(slice(0, HALF), None)
            if hh == 1:
                sums(slice(HALF, F), xr[d, rows])
            start(rsz(dirn, s, p))

    def brow(j, same):
        return remote(bs.at[j, same], br.at[j, same], br_s.at[j, same], br_r.at[j, same],
                      (row_at(j, 1), c))

    def backward(j):
        back_pass((j,), (2, 6, 3, 5, 4), False)
        for same in range(2):
            bs[j, same] = acc[j, :, TILE * same:TILE * (same + 1)].astype(jnp.bfloat16)
            if j:
                start(brow(j, same))

    corner_sums = remote(ns, nr, cn_s, cn_r, corner)

    def corner_product():
        @pl.when(at_corner)
        def _():
            ns[...] = jnp.dot(rows_of(corner[1]), nat[...].reshape(NM * TILE, F),
                              preferred_element_type=jnp.float32).astype(jnp.bfloat16)
            corner_sums.start()

    forward((3, 5))
    ag_step(3, 2)
    forward((2, 6))
    cross_sums(3)
    cross_sums(5)
    rs_step(2, 0)
    for p in range(2):
        ag_step(4, p)
    back_pass((3, 0), (1, 7), False)
    forward((1, 7))
    corner_product()
    share_wait(2, 6, 3, 5)

    @pl.when(at_corner)
    def _():
        corner_gather.wait_recv()
    backward(2)
    cross_sums(2)
    cross_sums(6)
    rs_step(2, 1)
    rs_step(2, 2)
    backward(1)
    cross_sums(1)
    cross_sums(7)
    rs_step(3, 0)
    backward(3)
    rs_step(3, 1)
    rs_step(3, 2)
    backward(0)
    forward((0,))
    rs_step(4, 0)
    cross_sums(0)
    rs_step(4, 1)
    rs_step(4, 2)

    def back_sum(same):
        value = acc[0, :, TILE * same:TILE * (same + 1)]
        for j in (1, 3, 2):
            brow(j, same).wait_recv()
            value = value + br[j, same].astype(jnp.float32)
        return value

    ls[...] = back_sum(0).astype(jnp.bfloat16)
    across = remote(ls, lr, lo_s, lo_r, lpartner)
    start(across)
    tile_copy.wait_recv()
    back = back_sum(1) + lax.dot_general(ht[opposite[1]], tr[...], (((1,), (1,)), ((), ())),
                                         preferred_element_type=jnp.float32)
    dd(0, 1).wait_recv()
    keep[0, 1] = keep[0, 1] + sib[0, 1]

    @pl.when(at_corner)
    def _():
        corner_sums.wait_recv()
        keep[0, 1] = keep[0, 1] + nr[...].astype(jnp.float32)
    for dirn in range(2):
        rsz(dirn, 4, 0).wait_recv()
    near = slice(0, HALF)
    hs[...] = (keep[0, 0, :, near] + sib[0, 0, :, near] + cr0[0, 3].astype(jnp.float32)
               + cr0[1, 3].astype(jnp.float32)).astype(jnp.bfloat16)
    cross = remote(hs, hr, hx_s, hx_r, hpartner)
    start(cross)
    across.wait_recv()
    keep[0, 1] = keep[0, 1] + (back + lr[...].astype(jnp.float32)).T
    xx(0).wait_recv()
    for p in (1, 2):
        for dirn in range(2):
            rsz(dirn, 4, p).wait_recv()
    summed = keep[0, 1] + cr1[0, 3].astype(jnp.float32) + cr1[1, 3].astype(jnp.float32)
    cross.wait_recv()
    summed = summed + jnp.concatenate([hr[...], xr[0]], axis=1).astype(jnp.float32)
    mixed = jnp.dot(summed, p_ref[...], precision=lax.Precision.HIGHEST,
                    preferred_element_type=jnp.float32)
    lifted = x_ref[...] + jnp.maximum(mixed, 0.0)
    scale = lax.rsqrt(jnp.mean(lifted * lifted, axis=-1, keepdims=True) + 1e-06)
    o_ref[...] = lifted * scale * g_ref[...]
    for copy in sends:
        copy.wait_send()

    @pl.when(at_corner)
    def _():
        corner_gather.wait_send()
        corner_sums.wait_send()


def shards(features, adjacency, tile_mask, projection, row_gain):
    vm = pl.BlockSpec(memory_space=pltpu.VMEM)
    bf, f32 = jnp.bfloat16, jnp.float32
    dma = pltpu.SemaphoreType.DMA
    out = pl.pallas_call(
        kernel,
        out_shape=jax.ShapeDtypeStruct((TILE, F), f32),
        in_specs=[vm, pl.BlockSpec(memory_space=pl.ANY),
                  pl.BlockSpec(memory_space=pltpu.SMEM), vm, vm],
        out_specs=vm,
        scratch_shapes=[
            pltpu.VMEM((NM, NK, TILE, TILE), bf),
            pltpu.VMEM((8, TILE, F), bf),
            pltpu.VMEM((NK, F, TILE), bf),
            pltpu.VMEM((8, 2, TILE, F), f32),
            pltpu.VMEM((8, 2, TILE, F), f32),
            pltpu.VMEM((8, 2, TILE, F), f32),
            pltpu.VMEM((2, 4, TILE, HALF), bf),
            pltpu.VMEM((2, 4, TILE, HALF), bf),
            pltpu.VMEM((2, 4, TILE, F), bf),
            pltpu.VMEM((2, 4, TILE, F), bf),
            pltpu.VMEM((8, TILE, F - HALF), bf),
            pltpu.VMEM((8, TILE, F - HALF), bf),
            pltpu.VMEM((TILE, HALF), bf),
            pltpu.VMEM((TILE, HALF), bf),
            pltpu.VMEM((4, F, 2 * TILE), f32),
            pltpu.VMEM((4, 2, F, TILE), bf),
            pltpu.VMEM((4, 2, F, TILE), bf),
            pltpu.VMEM((F, TILE), bf),
            pltpu.VMEM((F, TILE), bf),
            pltpu.VMEM((TILE, TILE), bf),
            pltpu.VMEM((TILE, TILE), bf),
            pltpu.VMEM((TILE, F), bf),
            pltpu.VMEM((TILE, F), bf),
            pltpu.SemaphoreType.REGULAR((4,)), dma, dma,
            dma((NM,)), dma((4, 2)), dma((4, 2)), dma, dma, dma((2, 4, 3)), dma((2, 4, 3)),
            dma, dma, dma((8,)), dma((8,)), dma((8, 2)), dma((8, 2)),
            dma((8, 2)), dma((8, 2)), dma((8,)), dma((8,)), dma((2, 4, 3)), dma((2, 4, 3)),
            dma, dma, dma((4, 2)), dma((4, 2)), dma, dma, dma, dma, dma, dma,
        ],
        compiler_params=pltpu.CompilerParams(
            collective_id=0, has_side_effects=True, vmem_limit_bytes=56 * 2**20),
        cost_estimate=pl.CostEstimate(
            flops=4 * 32 * 1024 * 128 * 512, bytes_accessed=9 * 2**20, transcendentals=128),
    )(features[0, 0], adjacency[:, 0, 0], tile_mask[:, 0, 0].T, projection[0], row_gain)
    return out[None, None]


def solution(mesh):
    return jax.shard_map(
        shards,
        mesh=mesh,
        in_specs=(
            P("col", "row", None, None),
            P(None, "row", "col", None, None, None),
            P(None, "row", "col", None),
            P(),
            P(),
        ),
        out_specs=P("col", "row", None, None),
        check_vma=False,
    )
```
